256 devices in a mesh: expert: 32 (over z, y), dp: 8 (over x, core).
Axes of the slice: x: 4, y: 4, z: 8, core: 2. Of those that a mesh axis runs over, the one named last changes fastest.
Arguments:
- tokens: bfloat16 [8192, 2048], P(('dp', 'expert')), may hold values from -6 to 6
- expert_ids: int32 [8192, 2], P(('dp', 'expert')), may hold values from 0 to 31, all different within a row; in each aligned block of 32 rows (0 to 31, 32 to 63, ...) at most 4 rows name the same one
- gates: float32 [8192, 2], P(('dp', 'expert')), may hold values from 0.1 to 1
- valid: int32 [8192], P(('dp', 'expert')), may hold values 0 or 1
- w_in: bfloat16 [32, 2048, 8192], P('expert', None, 'dp'), may hold values from -0.125 to 0.125
- w_out: bfloat16 [32, 8192, 2048], P('expert', 'dp'), may hold values from -0.0625 to 0.0625
- up_proj: bfloat16 [2048, 8192], P(None, 'expert'), may hold values from -0.125 to 0.125
- down_proj: bfloat16 [8192, 2048], P('expert'), may hold values from -0.0625 to 0.0625
Outputs:
- grad_up: float32 [2048, 8192], P('dp', 'expert')
- grad_down: float32 [8192, 2048], P('expert', 'dp')
The draws below stay inside these ranges and needn't reach their ends.
Inputs may be any that keep to these rules, and one draw needn't show every extreme that they name: `expert_ids`: the two experts of a token differ; among the 32 rows of one device no expert is named more than 4 times, a bound that some block reaches.
All inputs are finite; a program needn't handle non-finite values. No bound on the sum of `valid` on one device may be relied on, other than what follows from the above.
Results may differ from the reference program's by a relative error of at most 0.017.
Values may be sent and summed in bfloat16 or wider, within the bound.
A program may use at most 64 MiB of HBM per device.

```python
import math
import jax
import jax.numpy as jnp
import numpy as np
from jax import lax

D = 2048
FF = 8192
SFF = 8192
TOK_DEV = 32
EXPERTS = 32
CAP = 4
TOKENS = 8192
N_EXPERT = 32
N_DP = 8


def set_ends(array, own_key, low, top_value):
    longest = array.shape.index(max(array.shape))
    spots = []
    for shift in (0, 1):
        where = [jax.random.randint(jax.random.fold_in(own_key, axis), (), 0, length) for axis, length in enumerate(array.shape)]
        where[longest] = (where[longest] + shift) % array.shape[longest]
        spots.append(tuple(where))
    return array.at[spots[0]].set(low).at[spots[1]].set(top_value)


def levels(rng, extent, pieces, low, high):
    gain, own = 1.0, jax.random.fold_in(rng, 6)
    for axis_at, blocks in pieces:
        steps = jnp.exp(jax.random.uniform(jax.random.fold_in(own, axis_at), (blocks,), jnp.float32, low / len(pieces), high / len(pieces)))
        gain = gain * jnp.repeat(steps, extent[axis_at] // blocks).reshape([-1 if axis == axis_at else 1 for axis in range(len(extent))])
    return gain


def routed_block(rng, own, number, rows, number_of, top, limit, skew):
    ranking = jax.random.permutation(rng, number_of)
    heavy_load, common = shares(number_of, rows * top, limit, skew, True), shares(number_of, rows * top, limit, skew, False)
    places = jnp.arange(number_of)

    def named(sizes, rotation):
        used = int((sizes > 0).sum())
        fixed = max(1, used // 4)
        moved = fixed + (places - fixed + rotation * (used - fixed)) % max(1, number_of - fixed)
        return jnp.zeros((number_of,), jnp.int32).at[ranking[jnp.where(places < fixed, places, moved)]].set(jnp.asarray(sizes, jnp.int32))

    sizes = jnp.where(number % 4 == 0, named(heavy_load, number // 4), named(common, number - number // 4 - 1))
    mixed = jax.random.permutation(jax.random.fold_in(own, 3), number_of)
    source_of, sink = mixed[0:number_of // 2 * 2:2], mixed[1:number_of // 2 * 2:2]
    margin = jnp.minimum(sizes[source_of] - 1, limit - sizes[sink]) // 2
    margin = jnp.where((source_of == ranking[0]) | (sink == ranking[0]) | (sizes[sink] == 0), 0, jnp.maximum(margin, 0))
    moved = jax.random.randint(jax.random.fold_in(own, 4), (number_of // 2,), 0, 1 << 20) % (margin + 1)
    sizes = sizes.at[source_of].add(-moved).at[sink].add(moved)
    labels = jnp.searchsorted(jnp.cumsum(sizes), jnp.arange(rows * top), side="right").astype(jnp.int32)
    table = labels.reshape(top, rows).T
    table = table[jax.random.permutation(jax.random.fold_in(own, 1), rows)]
    rotation = jax.random.randint(jax.random.fold_in(own, 2), (rows, 1), 0, top)
    return jnp.take_along_axis(table, (jnp.arange(top)[None, :] + rotation) % top, axis=1)


def shares(count, total, bound, lean, full):
    weights = [(1 << 20) // math.isqrt(standing ** lean) + 1 for standing in range(1, count + 1)]
    largest = bound if full else min(bound, max(-(-total // count), total * weights[0] // sum(weights)))
    least = 1 if total - largest >= count - 1 else 0
    given, rest = [largest] + [least] * (count - 1), total - largest - least * (count - 1)
    while rest > 0:
        free = [i for i in range(1, count) if given[i] < largest] or [i for i in range(1, count) if given[i] < bound]
        pool, remaining = sum([weights[i] for i in free]), rest
        for i in free:
            addition = min(bound - given[i], max(1, remaining * weights[i] // pool), rest)
            given[i] = given[i] + addition
            rest = rest - addition
    return np.array(given)


def centred(stream_key, extent, width, reach, shards=(), kind=jnp.bfloat16):
    factor_of = levels(stream_key, extent, shards, -0.22, 0.18) if shards else 1.0
    result = jax.random.normal(stream_key, extent, jnp.float32) * width * factor_of
    return jnp.minimum(jnp.maximum(result, -reach), reach).astype(kind)


def setup_inputs(seed: int = 0) -> dict:
    seeds = jax.random.split(jax.random.key(seed), 9)
    tokens = centred(seeds[0], (TOKENS, D), 1.0, 6.0, ((0, 256),))
    expert_ids_keys = jax.random.split(jax.random.fold_in(seeds[1], 1), TOKENS // TOK_DEV)
    expert_ids_turns = jax.random.permutation(jax.random.fold_in(seeds[1], 3), TOKENS // TOK_DEV)
    expert_ids = jax.vmap(lambda own, number: routed_block(jax.random.fold_in(seeds[1], 2), own, number, TOK_DEV, EXPERTS, 2, CAP, 2))(expert_ids_keys, expert_ids_turns).reshape((TOKENS, 2))
    gates = jnp.clip(0.1 + 0.9 * jax.random.uniform(seeds[2], (TOKENS, 2), jnp.float32) ** levels(seeds[2], (TOKENS, 2), ((0, 256),), -0.2, 0.2), 0.1, 1.0)
    valid = set_ends((jax.random.randint(seeds[3], (TOKENS,), 0, 4) < 3).astype(jnp.int32), jax.random.fold_in(seeds[3], 1), 0, 1)
    w_in = centred(seeds[4], (EXPERTS, D, FF), D ** -0.5, 0.125, ((0, 32), (2, 8)))
    w_out = centred(seeds[5], (EXPERTS, FF, D), FF ** -0.5, 0.0625, ((0, 32), (1, 8)))
    up_proj = centred(seeds[6], (D, SFF), D ** -0.5, 0.125, ((1, 32),))
    down_proj = centred(seeds[7], (SFF, D), SFF ** -0.5, 0.0625, ((0, 32),))
    return dict(tokens=tokens, expert_ids=expert_ids, gates=gates, valid=valid, w_in=w_in, w_out=w_out, up_proj=up_proj, down_proj=down_proj)


def silu_grad(preact):
    sigmoid = jax.nn.sigmoid(preact)
    return sigmoid * (1.0 + preact * (1.0 - sigmoid))

def reference(tokens, expert_ids, gates, valid, w_in, w_out, up_proj, down_proj):
    n_blocks = TOKENS // TOK_DEV
    block_ids = expert_ids.reshape(n_blocks, TOK_DEV * 2)
    expert_hot = (block_ids[:, :, None] == jnp.arange(EXPERTS, dtype=jnp.int32)[None, None, :]).astype(jnp.int32)
    ranks = lax.optimization_barrier(jnp.sum((jnp.cumsum(expert_hot, axis=1) - 1) * expert_hot, axis=2))
    sources = jnp.arange(n_blocks, dtype=jnp.int32)[:, None]
    slot_rows = (sources * CAP + ranks).reshape(-1).astype(jnp.int32)
    token_index = jnp.repeat(jnp.arange(TOKENS, dtype=jnp.int32), 2)
    flat_ids = expert_ids.reshape(-1).astype(jnp.int32)
    table = jnp.full((EXPERTS, n_blocks * CAP), TOKENS, jnp.int32).at[flat_ids, slot_rows].set(token_index)
    gate_table = jnp.zeros((EXPERTS, n_blocks * CAP), jnp.float32).at[flat_ids, slot_rows].set(gates.reshape(-1))
    padded = jnp.concatenate([tokens, jnp.zeros((1, D), tokens.dtype)], axis=0)
    block_width = FF // N_DP

    def expert_step(target, inputs):
        slot_index, gate_col, inner_weight, outer_weight = inputs
        gathered = padded[slot_index]
        teacher_hidden = jax.nn.relu(jnp.dot(gathered, inner_weight, preferred_element_type=jnp.float32)).astype(jnp.bfloat16)
        summed = jnp.zeros((gathered.shape[0], D), jnp.float32)
        for part_index in range(N_DP):
            partial_value = jnp.dot(teacher_hidden[:, part_index * block_width:(part_index + 1) * block_width], outer_weight[part_index * block_width:(part_index + 1) * block_width], preferred_element_type=jnp.float32).astype(jnp.bfloat16)
            summed = summed + lax.optimization_barrier(partial_value).astype(jnp.float32)
        expert_out = lax.optimization_barrier(summed.astype(jnp.bfloat16)).astype(jnp.float32)
        return (target.at[slot_index].add(gate_col[:, None] * expert_out), None)
    target, _ = lax.scan(expert_step, jnp.zeros((TOKENS + 1, D), jnp.float32), (table, gate_table, w_in, w_out))
    target = target[:TOKENS]
    preact = jnp.dot(tokens, up_proj, preferred_element_type=jnp.float32)
    student_hidden = jax.nn.silu(preact).astype(jnp.bfloat16)
    student_block = SFF // N_EXPERT
    student_out = jnp.zeros((TOKENS, D), jnp.float32)
    for part_index in range(N_EXPERT):
        partial_value = jnp.dot(student_hidden[:, part_index * student_block:(part_index + 1) * student_block], down_proj[part_index * student_block:(part_index + 1) * student_block], preferred_element_type=jnp.float32).astype(jnp.bfloat16)
        student_out = student_out + lax.optimization_barrier(partial_value).astype(jnp.float32)
    scale = 1.0 / jnp.sqrt(jnp.float32(TOKENS))
    out_grad = (valid[:, None].astype(jnp.float32) * (student_out - target) * scale).astype(jnp.bfloat16)
    grad_down = lax.dot_general(student_hidden, out_grad, (((0,), (0,)), ((), ())), preferred_element_type=jnp.float32)
    back_hidden = lax.dot_general(out_grad, down_proj, (((1,), (1,)), ((), ())), preferred_element_type=jnp.float32)
    hidden_grad = (back_hidden * silu_grad(preact)).astype(jnp.bfloat16)
    grad_up = lax.dot_general(tokens, hidden_grad, (((0,), (0,)), ((), ())), preferred_element_type=jnp.float32)
    return (grad_up, grad_down)
```

```python
import jax
import jax.numpy as jnp
from jax import lax
from jax.sharding import PartitionSpec as P


def silu_grad(preact):
    sigmoid = jax.nn.sigmoid(preact)
    return sigmoid * (1.0 + preact * (1.0 - sigmoid))


def per_device(tokens, expert_ids, gates, valid, w_in, w_out, up_proj, down_proj):
    n_expert = lax.axis_size("expert")
    n_data = lax.axis_size("dp")
    tok_count = tokens.shape[0]
    capacity = 4 * tok_count // n_expert
    slot_width = n_expert * capacity
    flat_ids = expert_ids.reshape(-1)
    order = jnp.arange(flat_ids.shape[0], dtype=jnp.int32)
    earlier = (flat_ids[:, None] == flat_ids[None, :]) & (order[None, :] < order[:, None])
    ranks = jnp.sum(earlier.astype(jnp.int32), axis=1)
    slots = flat_ids * capacity + ranks
    slot_hot = (slots[:, None] == jnp.arange(slot_width, dtype=jnp.int32)[None, :]).astype(
        jnp.bfloat16
    )
    paired = slot_hot.reshape(tok_count, 2, slot_width)
    placing = paired[:, 0, :] + paired[:, 1, :]
    outgoing = lax.dot_general(
        placing, tokens, (((0,), (0,)), ((), ())), preferred_element_type=jnp.float32
    ).astype(jnp.bfloat16)
    stacked = lax.all_gather(
        outgoing.reshape(1, n_expert, capacity, tokens.shape[1]), "dp", axis=0, tiled=True
    )
    arrived = lax.all_to_all(stacked, "expert", split_axis=1, concat_axis=2, tiled=True)
    expert_rows = arrived.reshape(n_data * slot_width, tokens.shape[1])
    inner_weight = w_in[0]
    outer_weight = w_out[0]
    teacher_hidden = jax.nn.relu(
        jnp.dot(expert_rows, inner_weight, preferred_element_type=jnp.float32)
    ).astype(jnp.bfloat16)
    expert_out = lax.psum_scatter(
        jnp.dot(teacher_hidden, outer_weight, preferred_element_type=jnp.float32).astype(
            jnp.bfloat16
        ),
        "dp",
        scatter_dimension=0,
        tiled=True,
    )
    returned = lax.all_to_all(expert_out, "expert", split_axis=0, concat_axis=0, tiled=True)
    picked = jnp.dot(slot_hot, returned, preferred_element_type=jnp.float32).reshape(
        tok_count, 2, tokens.shape[1]
    )
    target = gates[:, 0:1] * picked[:, 0, :] + gates[:, 1:2] * picked[:, 1, :]
    group_tokens = lax.all_gather(tokens, "expert", axis=0, tiled=True)
    preact = jnp.dot(group_tokens, up_proj, preferred_element_type=jnp.float32)
    student_hidden = jax.nn.silu(preact).astype(jnp.bfloat16)
    partial_out = jnp.dot(student_hidden, down_proj, preferred_element_type=jnp.float32)
    student_out = lax.psum_scatter(
        partial_out.astype(jnp.bfloat16), "expert", scatter_dimension=0, tiled=True
    ).astype(jnp.float32)
    scale = 1.0 / jnp.sqrt(jnp.float32(tok_count * n_expert * n_data))
    out_grad = (valid[:, None].astype(jnp.float32) * (student_out - target) * scale).astype(
        jnp.bfloat16
    )
    group_grad = lax.all_gather(out_grad, "expert", axis=0, tiled=True)
    down_term = lax.dot_general(
        student_hidden, group_grad, (((0,), (0,)), ((), ())), preferred_element_type=jnp.float32
    )
    back_hidden = lax.dot_general(
        group_grad, down_proj, (((1,), (1,)), ((), ())), preferred_element_type=jnp.float32
    )
    hidden_grad = (back_hidden * silu_grad(preact)).astype(jnp.bfloat16)
    up_term = lax.dot_general(
        group_tokens, hidden_grad, (((0,), (0,)), ((), ())), preferred_element_type=jnp.float32
    )
    grad_up, grad_down = (
        lax.psum_scatter(
            up_term.astype(jnp.bfloat16), "dp", scatter_dimension=0, tiled=True
        ).astype(jnp.float32),
        lax.psum_scatter(
            down_term.astype(jnp.bfloat16), "dp", scatter_dimension=1, tiled=True
        ).astype(jnp.float32),
    )
    return (grad_up, grad_down)


def solution(mesh):
    return jax.shard_map(
        per_device,
        mesh=mesh,
        in_specs=(
            P(("dp", "expert"), None),
            P(("dp", "expert"), None),
            P(("dp", "expert"), None),
            P(("dp", "expert")),
            P("expert", None, "dp"),
            P("expert", "dp", None),
            P(None, "expert"),
            P("expert", None),
        ),
        out_specs=(P("dp", "expert"), P("expert", "dp")),
        check_vma=False,
    )
```

```python
import functools

import jax
import jax.numpy as jnp
from jax import lax
from jax.experimental import pallas as pl
from jax.experimental.pallas import tpu as pltpu
from jax.sharding import PartitionSpec as P

MESH = pl.DeviceIdType.MESH
CORES = 2
CAP = 4
LANES = 128
F32, BF16 = jnp.float32, jnp.bfloat16


def dot(a, b):
    return jnp.dot(a, b, preferred_element_type=F32)


def dot_nt(a, b):
    return lax.dot_general(a, b, (((1,), (1,)), ((), ())), preferred_element_type=F32)


def run_all(walks):
    walks = list(walks)
    while walks:
        for walk in list(walks):
            try:
                next(walk)
            except StopIteration:
                walks.remove(walk)


def kernel(
    nz, ny, nx, scale,
    tok_ref, ids_ref, gate_ref, valid_ref, win_hbm, wout_hbm, up_hbm, down_hbm,
    gup_ref, gdown_ref,
    win, wout, up, down, grp, rows, hid, part, part_in, xr, eout,
    hstu, hT, sgT, hgT, mix, zr, yr, zs, ys, og, gt, gt_in, gr,
    send_sem, recv_sem, load_sem,
):
    e, g = lax.axis_index("expert"), lax.axis_index("dp")
    z, y = e // ny, lax.rem(e, ny)
    x, c = g // CORES, lax.rem(g, CORES)
    tok, width = tok_ref.shape
    half = tok // 2
    group = nz * ny * tok
    slots = nz * ny * CAP
    hidden = hstu.shape[1]
    ffw = hid.shape[1]

    def at_z(k):
        return (lax.rem(z + k, nz) * ny + y, g)

    def at_y(k):
        return (z * ny + lax.rem(y + k, ny), g)

    def at_x(k):
        return (e, lax.rem(x + k, nx) * CORES + c)

    sibling = (e, x * CORES + 1 - c)

    loads = [
        pltpu.make_async_copy(up_hbm, up, load_sem.at[0]),
        pltpu.make_async_copy(win_hbm.at[0], win, load_sem.at[1]),
        pltpu.make_async_copy(wout_hbm.at[0], wout, load_sem.at[2]),
        pltpu.make_async_copy(down_hbm, down, load_sem.at[3]),
    ]
    for load in loads:
        load.start()

    barrier = pltpu.get_barrier_semaphore()
    near = [sibling]
    near += [at_z(k) for k in sorted({1, nz - 1})]
    near += [at_y(k) for k in range(1, ny)]
    near += [at_x(k) for k in sorted({1, nx - 1})]
    for device in near:
        pl.semaphore_signal(barrier, inc=1, device_id=device, device_id_type=MESH)

    lane = lax.broadcasted_iota(jnp.int32, (tok, LANES), 1)
    expert, kind = lane & 31, lane >> 5
    first, second = ids_ref[:, 0:1] == expert, ids_ref[:, 1:2] == expert
    hot = jnp.where(first | second, 1.0, 0.0)
    below = lax.broadcasted_iota(jnp.int32, (tok, tok), 1) < lax.broadcasted_iota(jnp.int32, (tok, tok), 0)
    rank = dot(jnp.where(below, 1.0, 0.0).astype(BF16), hot.astype(BF16))
    gate = jnp.where(first, gate_ref[:, 0:1], 0.0) + jnp.where(second, gate_ref[:, 1:2], 0.0)
    high = gate.astype(BF16).astype(F32)
    table = jnp.where(
        kind == 0, hot * (1.0 + rank), jnp.where(kind == 1, high, jnp.where(kind == 2, gate - high, 0.0))
    )
    grp[z, y, :, 0:width] = tok_ref[...]
    grp[z, y, :, width : width + LANES] = table.astype(BF16)

    pl.semaphore_wait(barrier, len(near))

    sent, count = [], [0]

    def send(src, dst, device):
        k = count[0]
        count[0] += 1
        copy = pltpu.make_async_remote_copy(
            src_ref=src, dst_ref=dst, send_sem=send_sem.at[k], recv_sem=recv_sem.at[k],
            device_id=device, device_id_type=MESH,
        )
        copy.start()
        sent.append(copy)
        return copy

    def ring_gather(n, i, way, at, region, arrived=None):
        last = None
        for s in range(1, n // 2 + 1):
            place = lax.rem(i + n - way * (s - 1), n)
            if last is not None:
                yield
                last.wait_recv()
                if arrived is not None:
                    arrived(place, None)
            cut = None if s < n // 2 else (0 if way == 1 else 1)
            ref = region(place, cut)
            last = send(ref, ref, at(1 if way == 1 else n - 1))
        yield
        last.wait_recv()
        if arrived is not None:
            arrived(lax.rem(i + n // 2, n), 0 if way == 1 else 1)

    def ring_sum(n, i, way, at, own, landing, add):
        last, cut = None, None
        for s in range(1, n // 2 + 1):
            place = lax.rem(i + n + way * (n // 2 - s + 1), n)
            if last is not None:
                yield
                last.wait_recv()
                add(own(place, cut), landing(s - 2, cut))
            cut = None if s > 1 else (0 if way == 1 else 1)
            last = send(own(place, cut), landing(s - 1, cut), at(1 if way == 1 else n - 1))
        yield
        last.wait_recv()
        add(own(i, cut), landing(n // 2 - 1, cut))

    def add_into(a, b):
        a[...] = (a[...].astype(F32) + b[...].astype(F32)).astype(BF16)

    def split(ref, cut, dim):
        if cut is None:
            return ref
        n = ref.shape[dim]
        low = n // 2 // LANES * LANES if dim == len(ref.shape) - 1 else n // 2
        where = pl.ds(0, low) if cut == 0 else pl.ds(low, n - low)
        return ref.at[tuple([slice(None)] * dim + [where])]

    upper, lower = pl.ds(0, half), pl.ds(half, half)

    def gather_plane(buf):
        def upper_first():
            mine = buf.at[z, y, upper, :]
            copies = [send(mine, mine, at_y(k)) for k in range(1, ny)]
            yield
            for copy in copies:
                copy.wait_recv()
            region = lambda p, cut: split(buf.at[p, :, upper, :], cut, 0)
            ways = [ring_gather(nz, z, w, at_z, region) for w in (1, -1)]
            yield from both(ways)

        def lower_first():
            region = lambda p, cut: split(buf.at[p, y, lower, :], cut, 1)
            yield from both([ring_gather(nz, z, w, at_z, region) for w in (1, -1)])
            region = lambda p, cut: split(buf.at[:, p, lower, :], cut, 0)
            yield from both([ring_gather(ny, y, w, at_y, region) for w in (1, -1)])

        run_all([upper_first(), lower_first()])

    def both(walks):
        while walks:
            for walk in list(walks):
                try:
                    next(walk)
                except StopIteration:
                    walks.remove(walk)
            if walks:
                yield

    with jax.named_scope("tokens_gather"):
        gather_plane(grp)

    tab = lambda: grp[:, :, :, width : width + LANES].reshape(group, LANES)
    with jax.named_scope("select"):
        pick = jnp.where(lax.broadcasted_iota(jnp.int32, (16, LANES), 1) == e, 1.0, 0.0).astype(BF16)
        ranks_row = dot_nt(pick, tab())[0:1, :]
        slot = lax.broadcasted_iota(jnp.int32, (slots, group), 0)
        token = lax.broadcasted_iota(jnp.int32, (slots, group), 1)
        wanted = ((slot & (CAP - 1)) + 1).astype(F32)
        chosen = (slot // CAP == token // tok) & (ranks_row == wanted)
        select = jnp.where(chosen, 1.0, 0.0).astype(BF16)
        tile = min(512, width)
        for j in range(width // tile):
            cols = slice(j * tile, (j + 1) * tile)
            rows[x, c, :, cols] = dot(select, grp[:, :, :, cols].reshape(group, tile)).astype(BF16)

    from_sibling = []

    def to_sibling(p, cut):
        ref = split(rows.at[p, c], cut, 0)
        from_sibling.append(send(ref, ref, sibling))

    to_sibling(x, None)
    gathers = [
        ring_gather(nx, x, w, at_x, lambda p, cut: split(rows.at[p, c], cut, 0), to_sibling) for w in (1, -1)
    ]
    for walk in gathers:
        next(walk)

    with jax.named_scope("student_forward"):
        loads[0].wait()
        step = 2 * ny * tok if nz % 2 == 0 else ny * tok

        @pl.loop(0, group // step)
        def _(k):
            block = grp[pl.ds(k * (step // (ny * tok)), step // (ny * tok)), :, :, 0:width].reshape(step, width)
            value = dot(block, up[...])
            place = pl.multiple_of(k * step, step)
            sig = jax.nn.sigmoid(value)
            hstu[pl.ds(place, step), :] = (value * sig).astype(BF16)
            hT[:, pl.ds(place, step)] = (value * sig).T.astype(BF16)
            sgT[:, pl.ds(place, step)] = (sig * (1.0 + value * (1.0 - sig))).T

    loads[1].wait()
    loads[2].wait()

    def teacher(p):
        tile = min(256, ffw)

        @pl.loop(0, ffw // tile)
        def _(j):
            cols = pl.ds(pl.multiple_of(j * tile, tile), tile)
            value = dot(rows[p].reshape(CORES * slots, width), win[:, cols])
            hid[:, cols] = jnp.maximum(value, 0.0).astype(BF16)

        tile2 = min(256, width)

        @pl.loop(0, width // tile2)
        def _(j):
            cols = pl.ds(pl.multiple_of(j * tile2, tile2), tile2)
            value = dot(hid[...], wout[:, cols])
            part[p, :, :, cols] = value.astype(BF16).reshape(CORES, slots, tile2)

    with jax.named_scope("teacher"):
        run_all(gathers)
        for copy in from_sibling:
            copy.wait_recv()
        order = [lax.rem(x + k, nx) for k in ([nx // 2] + [k for k in range(1, nx) if k != nx // 2] + [0])]
        swaps = []
        for p in order:
            teacher(p)
            swaps.append(send(part.at[p, 1 - c], part_in.at[p], sibling))
        for p, swap in zip(order, swaps):
            swap.wait_recv()
            add_into(part.at[p, c], part_in.at[p])
        run_all([
            ring_sum(
                nx, x, w, at_x, lambda p, cut: split(part.at[p, c], cut, 0),
                lambda s, cut, w=w: split(xr.at[(1 - w) // 2, s], cut, 0), add_into,
            )
            for w in (1, -1)
        ])
        eout[...] = part[x, c]

    with jax.named_scope("combine"):
        loads[3].wait()
        blocks = step // (ny * tok)
        tile = min(512, width)
        row = lax.broadcasted_iota(jnp.int32, (LANES, slots), 0)
        pick_rank = jnp.where(row == e, 1.0, 0.0).astype(BF16)
        pick_gate = jnp.where((row == e + 32) | (row == e + 64), 1.0, 0.0).astype(BF16)

        @pl.loop(0, group // step)
        def _(k):
            tab_k = grp[pl.ds(k * blocks, blocks), :, :, width : width + LANES].reshape(step, LANES)
            ranks = dot(tab_k, pick_rank)
            gates = dot(tab_k, pick_gate)
            token = lax.broadcasted_iota(jnp.int32, (step, slots), 0) + k * step
            slot = lax.broadcasted_iota(jnp.int32, (step, slots), 1)
            chosen = (slot // CAP == token // tok) & (ranks == ((slot & (CAP - 1)) + 1).astype(F32))
            back = jnp.where(chosen, 1.0, 0.0).astype(BF16)
            place = pl.multiple_of(k * step, step)
            for j in range(width // tile):
                cols = slice(j * tile, (j + 1) * tile)
                value = dot(hstu[pl.ds(place, step), :], down[:, cols])
                value = value - gates[:, 0:1] * dot(back, eout[:, cols])
                mix[pl.ds(k * blocks, blocks), :, :, cols] = value.astype(BF16).reshape(blocks, ny, tok, tile)

    def sum_upper():
        yield from both([
            ring_sum(
                nz, z, w, at_z, lambda p, cut: split(mix.at[p, :, upper, :], cut, 0),
                lambda s, cut, w=w: split(zr.at[(1 - w) // 2, s], cut, 0), add_into,
            )
            for w in (1, -1)
        ])
        copies = []
        for k in range(1, ny):
            to = lax.rem(y + k, ny)
            copies.append(send(mix.at[z, to, upper, :], ys.at[k - 1], at_y(k)))
        yield
        for copy in copies:
            copy.wait_recv()

    def sum_lower():
        yield from both([
            ring_sum(
                ny, y, w, at_y, lambda p, cut: split(mix.at[:, p, lower, :], cut, 0),
                lambda s, cut, w=w: split(yr.at[(1 - w) // 2, s], cut, 0), add_into,
            )
            for w in (1, -1)
        ])
        yield from both([
            ring_sum(
                nz, z, w, at_z, lambda p, cut: split(mix.at[p, y, lower, :], cut, 1),
                lambda s, cut, w=w: split(zs.at[(1 - w) // 2, s], cut, 1), add_into,
            )
            for w in (1, -1)
        ])

    with jax.named_scope("output_sum"):
        run_all([sum_upper(), sum_lower()])
        weight = valid_ref[...].astype(F32) * scale
        value = mix[z, y, 0:half, :].astype(F32)
        for k in range(ny - 1):
            value = value + ys[k].astype(F32)
        og[z, y, 0:half, :] = (weight[0:half] * value).astype(BF16)
        og[z, y, half:tok, :] = (weight[half:tok] * mix[z, y, half:tok, :].astype(F32)).astype(BF16)

    with jax.named_scope("grad_gather"):
        gather_plane(og)

    with jax.named_scope("backward"):
        share = width // (nx * CORES)

        @pl.loop(0, nx * CORES)
        def _(k):
            cols = pl.ds(pl.multiple_of(k * share, share), share)
            value = dot(hT[...], og[:, :, :, cols].reshape(group, share))
            gt[k // CORES, lax.rem(k, CORES), 1] = value.astype(BF16)

        swap_down = send(gt.at[:, 1 - c, 1], gt_in.at[:, 1], sibling)

        @pl.loop(0, group // step)
        def _(k):
            block = og[pl.ds(k * blocks, blocks)].reshape(step, width)
            place = pl.ds(pl.multiple_of(k * step, step), step)
            hgT[:, place] = (dot_nt(down[...], block) * sgT[:, place]).astype(BF16)

        @pl.loop(0, nx * CORES)
        def _(k):
            cols = pl.ds(pl.multiple_of(k * share, share), share)
            value = dot(hgT[...], grp[:, :, :, cols].reshape(group, share))
            gt[k // CORES, lax.rem(k, CORES), 0] = value.astype(BF16)

        swap_up = send(gt.at[:, 1 - c, 0], gt_in.at[:, 0], sibling)
        swap_down.wait_recv()
        swap_up.wait_recv()
        for p in range(nx):
            add_into(gt.at[p, c], gt_in.at[p])
        run_all([
            ring_sum(
                nx, x, w, at_x, lambda p, cut: split(gt.at[p, c], cut, 0),
                lambda s, cut, w=w: split(gr.at[(1 - w) // 2, s], cut, 0), add_into,
            )
            for w in (1, -1)
        ])
        gup_ref[...] = gt[x, c, 0].astype(F32).T
        gdown_ref[...] = gt[x, c, 1].astype(F32)

    for copy in sent:
        copy.wait_send()


def per_device(nz, ny, nx, tokens, expert_ids, gates, valid, w_in, w_out, up_proj, down_proj):
    tok, width = tokens.shape
    ffw, hidden = w_in.shape[2], up_proj.shape[1]
    group = nz * ny * tok
    slots = nz * ny * CAP
    half = tok // 2
    share = width // (nx * CORES)
    scale = 1.0 / float(group * nx * CORES) ** 0.5
    copies = 160
    vmem = lambda shape, dtype=BF16: pltpu.VMEM(shape, dtype)
    scratch = [
        vmem((width, ffw)), vmem((ffw, width)), vmem((width, hidden)), vmem((hidden, width)),
        vmem((nz, ny, tok, width + LANES)),
        vmem((nx, CORES, slots, width)),
        vmem((CORES * slots, ffw)),
        vmem((nx, CORES, slots, width)),
        vmem((nx, slots, width)),
        vmem((2, nx // 2, slots, width)),
        vmem((slots, width)),
        vmem((group, hidden)),
        vmem((hidden, group)), vmem((hidden, group), F32), vmem((hidden, group)),
        vmem((nz, ny, tok, width)),
        vmem((2, nz // 2, ny, half, width)),
        vmem((2, ny // 2, nz, half, width)),
        vmem((2, nz // 2, half, width)),
        vmem((max(ny - 1, 1), half, width)),
        vmem((nz, ny, tok, width)),
        vmem((nx, CORES, 2, hidden, share)),
        vmem((nx, 2, hidden, share)),
        vmem((2, nx // 2, 2, hidden, share)),
        pltpu.SemaphoreType.DMA((copies,)),
        pltpu.SemaphoreType.DMA((copies,)),
        pltpu.SemaphoreType.DMA((4,)),
    ]
    in_vmem = pl.BlockSpec(memory_space=pltpu.VMEM)
    anywhere = pl.BlockSpec(memory_space=pl.ANY)
    return pl.pallas_call(
        functools.partial(kernel, nz, ny, nx, scale),
        out_shape=(
            jax.ShapeDtypeStruct((share, hidden), F32),
            jax.ShapeDtypeStruct((hidden, share), F32),
        ),
        in_specs=[in_vmem] * 4 + [anywhere] * 4,
        out_specs=(in_vmem, in_vmem),
        scratch_shapes=scratch,
        cost_estimate=pl.CostEstimate(flops=15 * 10**9, bytes_accessed=11 * 10**6, transcendentals=0),
        compiler_params=pltpu.CompilerParams(
            collective_id=0, has_side_effects=True, vmem_limit_bytes=60 * 2**20
        ),
    )(tokens, expert_ids, gates, valid.reshape(tok, 1), w_in, w_out, up_proj, down_proj)


def solution(mesh):
    n_expert, n_dp = mesh.shape["expert"], mesh.shape["dp"]
    ny = 4 if n_expert >= 16 else 2
    nz, nx = n_expert // ny, n_dp // CORES
    return jax.shard_map(
        functools.partial(per_device, nz, ny, nx),
        mesh=mesh,
        in_specs=(
            P(("dp", "expert"), None),
            P(("dp", "expert"), None),
            P(("dp", "expert"), None),
            P(("dp", "expert")),
            P("expert", None, "dp"),
            P("expert", "dp", None),
            P(None, "expert"),
            P("expert", None),
        ),
        out_specs=(P("dp", "expert"), P("expert", "dp")),
        check_vma=False,
    )
```

```python
import functools

import jax
import jax.numpy as jnp
from jax import lax
from jax.experimental import pallas as pl
from jax.experimental.pallas import tpu as pltpu
from jax.sharding import PartitionSpec as P

MESH = pl.DeviceIdType.MESH
CORES = 2
CAP = 4
LANES = 128
Z_FIRST = 0
F32, BF16 = jnp.float32, jnp.bfloat16


def dot(a, b):
    return jnp.dot(a, b, preferred_element_type=F32)


def dot_nt(a, b):
    return lax.dot_general(a, b, (((1,), (1,)), ((), ())), preferred_element_type=F32)


class Event:
    def __init__(self):
        self.done = False


class Work:
    def __init__(self, us, rank=0):
        self.us, self.rank = us, rank


class Plan:
    RATE, INNER, LATENCY = 100e3, 400e3, 2.2

    def __init__(self):
        self.now, self.busy, self.processes = 0.0, {}, []

    def transfer(self, link, nbytes):
        start = max(self.now, self.busy.get(link, 0.0))
        self.busy[link] = start + nbytes / (self.INNER if link == "core" else self.RATE / CORES)
        return self.busy[link] + self.LATENCY

    def spawn(self, process):
        self.processes.append([process, self.now])

    def run(self):
        while self.processes:
            ready, works, later = [], [], []
            for i, (_, want) in enumerate(self.processes):
                if isinstance(want, Event):
                    if want.done:
                        ready.append((self.now, i))
                elif isinstance(want, Work):
                    works.append((want.rank, i))
                elif want <= self.now:
                    ready.append((want, i))
                else:
                    later.append((want, i))
            if ready:
                i = min(ready)[1]
            elif works:
                i = min(works)[1]
                self.now += self.processes[i][1].us
            else:
                self.now, i = min(later)
            process = self.processes[i]
            try:
                process[1] = next(process[0])
            except StopIteration:
                self.processes.remove(process)


def add_into(a, b):
    a[...] = (a[...].astype(F32) + b[...].astype(F32)).astype(BF16)


def kernel(
    nz, ny, nx, scale, n_part,
    tok_ref, ids_ref, gate_ref, valid_ref, win_hbm, wout_hbm, up_hbm, down_hbm,
    gup_ref, gdown_ref,
    win, wout, up, down, grp, rows, acc, hid, part, part_in, xr, eout,
    hstu, hT, sgT, hgT, back, mix, zr, yr, zs, ys, og, gt, gt_in, gr,
    send_sem, recv_sem, load_sem,
):
    e, g = lax.axis_index("expert"), lax.axis_index("dp")
    z, y = e // ny, lax.rem(e, ny)
    x, c = g // CORES, lax.rem(g, CORES)
    tok, width = tok_ref.shape
    group = nz * ny * tok
    slots = nz * ny * CAP
    ffw = win.shape[1]
    wide = width // n_part
    share = width // (nx * CORES)

    def at_z(k):
        return (lax.rem(z + k, nz) * ny + y, g)

    def at_y(k):
        return (z * ny + lax.rem(y + k, ny), g)

    def at_x(k):
        return (e, lax.rem(x + k, nx) * CORES + c)

    sibling = (e, x * CORES + 1 - c)
    ring_z, ring_y, ring_x = (nz, z, at_z, "z"), (ny, y, at_y, "y"), (nx, x, at_x, "x")

    loads = [
        pltpu.make_async_copy(win_hbm.at[0], win, load_sem.at[0]),
        pltpu.make_async_copy(up_hbm, up, load_sem.at[1]),
        pltpu.make_async_copy(wout_hbm.at[0], wout, load_sem.at[2]),
        pltpu.make_async_copy(down_hbm, down, load_sem.at[3]),
    ]

    barrier = pltpu.get_barrier_semaphore()
    near = [sibling]
    near += [at_z(k) for k in sorted({1, nz - 1})]
    near += [at_y(k) for k in range(1, ny)]
    near += [at_x(k) for k in sorted({1, nx - 1})]
    for device in near:
        pl.semaphore_signal(barrier, inc=1, device_id=device, device_id_type=MESH)
    for load in loads:
        load.start()

    row = lax.broadcasted_iota(jnp.int32, (LANES, tok), 0)
    expert, kind = row & 31, row >> 5
    first, second = ids_ref[0:1, :] == expert, ids_ref[1:2, :] == expert
    hot = jnp.where(first | second, 1.0, 0.0)
    before = lax.broadcasted_iota(jnp.int32, (tok, tok), 0) < lax.broadcasted_iota(jnp.int32, (tok, tok), 1)
    rank = dot(hot.astype(BF16), jnp.where(before, 1.0, 0.0).astype(BF16))
    gate = jnp.where(first, gate_ref[0:1, :], 0.0) + jnp.where(second, gate_ref[1:2, :], 0.0)
    high = gate.astype(BF16).astype(F32)
    table = jnp.where(kind == 0, hot * (1.0 + rank), jnp.where(kind == 1, high, gate - high))
    table = jnp.where(kind == 3, valid_ref[...].astype(F32), table)
    grp[z, y, :, 0:LANES] = table.T.astype(BF16)
    grp[z, y, :, LANES : LANES + width] = tok_ref[...]

    pl.semaphore_wait(barrier, len(near))

    plan = Plan()
    sent = []

    def send(src, dst, device, link):
        k = len(sent)
        copy = pltpu.make_async_remote_copy(
            src_ref=src, dst_ref=dst, send_sem=send_sem.at[k], recv_sem=recv_sem.at[k],
            device_id=device, device_id_type=MESH,
        )
        copy.start()
        size = 2
        for n in src.shape:
            size *= n
        sent.append(copy)
        return copy, plan.transfer(link, size)

    def ring_gather(ring, way, region, done, far, arrived=None):
        n, i, at, name = ring
        steps = n // 2 if way == far else n // 2 - 1
        for s in range(1, steps + 1):
            ref = region(lax.rem(i + n - way * (s - 1), n))
            copy, due = send(ref, ref, at(1 if way == 1 else n - 1), name + str(way))
            yield due
            copy.wait_recv()
            if arrived is not None:
                arrived(way * s)
        done.done = True

    def ring_sum(ring, way, own, landing, done, far, us):
        n, i, at, name = ring
        steps = n // 2 if way == far else n // 2 - 1
        for s in range(1, steps + 1):
            place = lax.rem(i + n + way * (steps - s + 1), n)
            copy, due = send(own(place), landing(s - 1), at(1 if way == 1 else n - 1), name + str(way))
            yield due
            copy.wait_recv()
            add_into(own(lax.rem(i + n + way * (steps - s), n)), landing(s - 1))
            plan.now += us
        done.done = True

    def both_ways(start):
        ends = []
        for way in (1, -1):
            ends.append(Event())
            plan.spawn(start(way, ends[-1]))
        return ends

    def all_of(events, done):
        for event in events:
            yield event
        done.done = True

    def y_then_z(buf, cols, done):
        ends = []

        def along_z(k):
            far = 1 if k in (0, 1) else -1
            region = lambda p: buf.at[p, lax.rem(y + ny - k, ny), :, cols]
            ends.extend(both_ways(lambda w, end: ring_gather(ring_z, w, region, end, far)))

        mine = buf.at[z, y, :, cols]
        hops = sorted(range(1, ny), key=lambda k: min(k, ny - k))
        copies = [(k, *send(mine, mine, at_y(k), "y1" if k <= ny // 2 else "y-1")) for k in hops]
        along_z(0)
        for k, copy, due in copies:
            yield due
            copy.wait_recv()
            along_z(k)
        plan.spawn(all_of(ends, done))

    def z_then_y(buf, cols, done):
        ends = []

        def along_y(k):
            far = 1 if len(ends) % 4 == 0 else -1
            region = lambda p: buf.at[lax.rem(z + nz - k, nz), p, :, cols]
            ends.extend(both_ways(lambda w, end: ring_gather(ring_y, w, region, end, far)))

        region = lambda p: buf.at[p, y, :, cols]
        firsts = both_ways(lambda w, end: ring_gather(ring_z, w, region, end, 1, along_y))
        along_y(0)
        for end in firsts:
            yield end
        plan.spawn(all_of(ends, done))

    def columns(q, shift):
        return pl.ds(q * wide + (shift if q else 0), wide + (0 if q else shift))

    def gather_plane(buf, q, shift, done):
        return (z_then_y if q == Z_FIRST else y_then_z)(buf, columns(q, shift), done)

    def sum_z_then_y(q, cols, done):
        from_y = []

        def along_z(k):
            to = lax.rem(y + k, ny)
            own = lambda p: mix.at[p, to, :, cols]
            landing = lambda w: lambda s: zr.at[k, (1 - w) // 2, s]
            far = 1 if k in (0, 1) else -1
            for end in both_ways(lambda w, end: ring_sum(ring_z, w, own, landing(w), end, far, 0.1)):
                yield end
            if k:
                from_y.append(
                    send(mix.at[z, to, :, cols], ys.at[k - 1], at_y(k), "y1" if k <= ny // 2 else "y-1")
                )
            finished[k].done = True

        finished = [Event() for _ in range(ny)]
        for k in sorted(range(ny), key=lambda k: -min(k, ny - k)):
            plan.spawn(along_z(k))
        for event in finished:
            yield event
        for copy, due in from_y:
            yield due
            copy.wait_recv()
        done.done = True

    def sum_y_then_z(q, cols, done):
        finished = [Event() for _ in range(nz)]

        def along_y(k, far):
            to = lax.rem(z + k, nz)
            own = lambda p: mix.at[to, p, :, cols]
            landing = lambda w: lambda s: yr.at[k, (1 - w) // 2, s]
            for end in both_ways(lambda w, end: ring_sum(ring_y, w, own, landing(w), end, far, 0.1)):
                yield end
            finished[k].done = True

        def along_z(way, end):
            n, i, at, name = ring_z
            steps = n // 2 if way == 1 else n // 2 - 1
            for s in range(1, steps + 1):
                k = steps - s + 1
                yield finished[(way * k) % n]
                copy, due = send(
                    mix.at[lax.rem(i + n + way * k, n), y, :, cols], zs.at[(1 - way) // 2, s - 1],
                    at(1 if way == 1 else n - 1), name + str(way),
                )
                yield due
                copy.wait_recv()
                yield finished[(way * (k - 1)) % n]
                add_into(mix.at[lax.rem(i + n + way * (k - 1), n), y, :, cols], zs.at[(1 - way) // 2, s - 1])
                plan.now += 0.1
            end.done = True

        for at, k in enumerate(sorted(range(nz), key=lambda k: -min(k, nz - k))):
            plan.spawn(along_y(k, 1 if at % 2 == 0 else -1))
        for end in both_ways(along_z):
            yield end
        done.done = True

    each = lambda: [Event() for _ in range(n_part)]
    gathered, selected, hidden, summed, mixed, out, grads = each(), each(), each(), each(), each(), each(), each()
    student = Event()
    part_cols = lambda q: pl.ds(q * wide, wide)
    hops = nx // 2
    order = [nx // 2] + [k for k in range(1, nx) if k != nx // 2] + [0]
    whole = [[Event() for _ in range(nx)] for _ in range(n_part)]
    multiplied = [[Event() for _ in range(nx)] for _ in range(n_part)]

    def take_slots(q):
        if q:
            yield selected[q - 1]
        yield gathered[q]
        pick = jnp.where(lax.broadcasted_iota(jnp.int32, (16, LANES), 1) == e, 1.0, 0.0).astype(BF16)
        ranks_row = dot_nt(pick, grp[:, :, :, 0:LANES].reshape(group, LANES))[0:1, :]
        slot = lax.broadcasted_iota(jnp.int32, (slots, group), 0)
        token = lax.broadcasted_iota(jnp.int32, (slots, group), 1)
        chosen = (slot // CAP == token // tok) & (ranks_row == ((slot & (CAP - 1)) + 1).astype(F32))
        select = jnp.where(chosen, 1.0, 0.0).astype(BF16)
        tile = min(512, wide)
        for j in range(wide // tile):
            at = q * wide + j * tile
            block = grp[:, :, :, LANES + at : LANES + at + tile].reshape(group, tile)
            rows[x, c, :, at : at + tile] = dot(select, block).astype(BF16)
        plan.now += 0.6
        selected[q].done = True
        cols = part_cols(q)
        fromsib = {k: [] for k in range(nx)}
        low, high = pl.ds(0, slots // 2), pl.ds(slots // 2, slots // 2)

        def to_sibling(k, p, where):
            ref = rows.at[p, c, where, cols]
            fromsib[k].append(send(ref, ref, sibling, "core"))
            if len(fromsib[k]) == (2 if k else 1):
                plan.spawn(settle(k))

        def settle(k):
            for copy, due in fromsib[k]:
                yield due
                copy.wait_recv()
            whole[q][k].done = True

        to_sibling(0, x, pl.ds(0, slots))
        for where, far in ((low, 1), (high, -1)):
            region = lambda p, where=where: rows.at[p, c, where, cols]
            both_ways(
                lambda w, end, where=where, region=region, far=far: ring_gather(
                    ring_x, w, region, end, far,
                    lambda d, where=where: to_sibling(d % nx, lax.rem(x + nx - d, nx), where),
                )
            )

    def place_of(k):
        return lax.rem(x + nx - k, nx)

    def first_product(q):
        for k in [0] + [k for k in range(1, nx) if k != hops] + [hops]:
            yield whole[q][k]
            if q:
                yield multiplied[q - 1][k]
            yield Work(1.4)
            if q == 0 and k == 0:
                loads[0].wait()
            p = place_of(k)
            tile = min(256, ffw)

            @pl.loop(0, ffw // tile)
            def _(j):
                cols = pl.ds(pl.multiple_of(j * tile, tile), tile)
                value = dot(
                    rows[p, :, :, part_cols(q)].reshape(CORES * slots, wide), win[part_cols(q), cols]
                ).reshape(CORES, slots, tile)
                if q:
                    value = value + acc[p, :, :, cols]
                if q < n_part - 1:
                    acc[p, :, :, cols] = value
                else:
                    hid[p, :, :, cols] = jnp.maximum(value, 0.0).astype(BF16)

            multiplied[q][k].done = True
        hidden[q].done = True

    def second_product(q):
        yield hidden[n_part - 1]
        if q:
            yield Work(0.0, q)
        if q == 0:
            loads[2].wait()
        tile = min(256, wide)
        for j in range(wide // tile):
            yield Work(1.0, q)
            cols = pl.ds(q * wide + j * tile, tile)
            value = dot(hid[...].reshape(nx * CORES * slots, ffw), wout[:, cols])
            part[:, :, :, cols] = value.astype(BF16).reshape(nx, CORES, slots, tile)
        cols = part_cols(q)
        swaps = []
        for k in order:
            p = lax.rem(x + k, nx)
            swaps.append(send(part.at[p, 1 - c, :, cols], part_in.at[p, :, cols], sibling, "core"))
        for k, (copy, due) in zip(order, swaps):
            p = lax.rem(x + k, nx)
            yield due
            copy.wait_recv()
            add_into(part.at[p, c, :, cols], part_in.at[p, :, cols])
        ends = []
        for h, far in ((0, 1), (1, -1)):
            where = pl.ds(h * (slots // 2), slots // 2)
            own = lambda p, where=where: part.at[p, c, where, cols]
            landing = lambda w, where=where: lambda s: xr.at[q, (1 - w) // 2, s, where]
            ends += both_ways(
                lambda w, end, own=own, landing=landing, far=far: ring_sum(
                    ring_x, w, own, landing(w), end, far, 0.15
                )
            )
        for end in ends:
            yield end
        eout[:, cols] = part[x, c, :, cols]
        summed[q].done = True

    blocks = 2 if nz % 2 == 0 else 1
    step = blocks * ny * tok

    def student_forward():
        for event in gathered:
            yield event
        loads[1].wait()
        for k in range(group // step):
            yield Work(1.0, 5)
            at = k * step
            block = grp[k * blocks : (k + 1) * blocks, :, :, LANES : LANES + width].reshape(step, width)
            value = dot(block, up[...])
            sig = jax.nn.sigmoid(value)
            act = value * sig
            hstu[at : at + step, :] = act.astype(BF16)
            hT[:, at : at + step] = act.T.astype(BF16)
            sgT[:, at : at + step] = (sig * (1.0 + value * (1.0 - sig))).T
        student.done = True

    def combine(q):
        yield student
        yield summed[q]
        if q == 0:
            loads[3].wait()
        tile = min(512, wide)
        line = lax.broadcasted_iota(jnp.int32, (LANES, slots), 0)
        pick_rank = jnp.where(line == e, 1.0, 0.0).astype(BF16)
        pick_gate = jnp.where((line == e + 32) | (line == e + 64), 1.0, 0.0).astype(BF16)

        @pl.loop(0, group // step)
        def _(k):
            tab = grp[pl.ds(k * blocks, blocks), :, :, 0:LANES].reshape(step, LANES)
            ranks = dot(tab, pick_rank)
            gates = dot(tab, pick_gate)
            token = lax.broadcasted_iota(jnp.int32, (step, slots), 0) + k * step
            slot = lax.broadcasted_iota(jnp.int32, (step, slots), 1)
            chosen = (slot // CAP == token // tok) & (ranks == ((slot & (CAP - 1)) + 1).astype(F32))
            spread = jnp.where(chosen, 1.0, 0.0).astype(BF16)
            at = pl.multiple_of(k * step, step)
            for j in range(wide // tile):
                cols = slice(q * wide + j * tile, q * wide + (j + 1) * tile)
                value = dot(hstu[pl.ds(at, step), :], down[:, cols])
                value = value - gates[:, 0:1] * dot(spread, eout[:, cols])
                mix[pl.ds(k * blocks, blocks), :, :, cols] = value.astype(BF16).reshape(blocks, ny, tok, tile)

        plan.now += 1.7
        cols, end = columns(q, 0), Event()
        plan.spawn((sum_y_then_z if q == Z_FIRST else sum_z_then_y)(q, cols, end))
        yield end
        value = mix[z, y, :, cols].astype(F32)
        if q != Z_FIRST:
            for k in range(ny - 1):
                value = value + ys[k].astype(F32)
        og[z, y, :, cols] = (grp[z, y, :, 96:97].astype(F32) * scale * value).astype(BF16)
        plan.now += 0.3
        plan.spawn(gather_plane(og, q, 0, grads[q]))

    def to_places(kind):
        swap, due = send(gt.at[kind, :, 1 - c], gt_in.at[kind], sibling, "core")
        yield due
        swap.wait_recv()
        for p in range(nx):
            add_into(gt.at[kind, p, c], gt_in.at[kind, p])
        n = gt.shape[3]
        ends = []
        for h, far in ((0, 1), (1, -1)):
            where = pl.ds(h * (n // 2), n // 2)
            own = lambda p, where=where: gt.at[kind, p, c, where]
            landing = lambda w, where=where: lambda s: gr.at[kind, (1 - w) // 2, s, where]
            ends += both_ways(
                lambda w, end, own=own, landing=landing, far=far: ring_sum(
                    ring_x, w, own, landing(w), end, far, 0.05
                )
            )
        for end in ends:
            yield end
        if kind:
            gdown_ref[...] = gt[1, x, c].astype(F32)
        else:
            gup_ref[...] = gt[0, x, c].astype(F32).T

    def backward():
        per_part = nx * CORES // n_part
        for q in range(n_part):
            yield grads[q]
            yield Work(1.2)

            @pl.loop(0, per_part)
            def _(k):
                to = q * per_part + k
                cols = pl.ds(pl.multiple_of(to * share, share), share)
                value = dot(hT[...], og[:, :, :, cols].reshape(group, share))
                gt[1, to // CORES, lax.rem(to, CORES)] = value.astype(BF16)

            if q == n_part - 1:
                plan.spawn(to_places(1))
            yield Work(1.2)

            @pl.loop(0, group // step)
            def _(k):
                block = og[pl.ds(k * blocks, blocks), :, :, part_cols(q)].reshape(step, wide)
                place = pl.ds(pl.multiple_of(k * step, step), step)
                value = dot_nt(down[:, part_cols(q)], block)
                if q:
                    value = value + back[:, place]
                if q < n_part - 1:
                    back[:, place] = value
                else:
                    hgT[:, place] = (value * sgT[:, place]).astype(BF16)

        yield Work(2.2)

        @pl.loop(0, nx * CORES)
        def _(k):
            cols = pl.ds(pl.multiple_of(LANES + k * share, LANES), share)
            value = dot(hgT[...], grp[:, :, :, cols].reshape(group, share))
            gt[0, k // CORES, lax.rem(k, CORES)] = value.astype(BF16)

        plan.spawn(to_places(0))

    for q in range(n_part):
        plan.spawn(gather_plane(grp, q, LANES, gathered[q]))
        plan.spawn(take_slots(q))
        plan.spawn(first_product(q))
        plan.spawn(second_product(q))
        plan.spawn(combine(q))
    plan.spawn(student_forward())
    plan.spawn(backward())
    plan.run()

    for copy in sent:
        copy.wait_send()


def per_device(nz, ny, nx, tokens, expert_ids, gates, valid, w_in, w_out, up_proj, down_proj):
    tok, width = tokens.shape
    ffw, hidden = w_in.shape[2], up_proj.shape[1]
    group = nz * ny * tok
    slots = nz * ny * CAP
    share = width // (nx * CORES)
    scale = 1.0 / float(group * nx * CORES) ** 0.5
    n_part = 2
    wide = width // n_part
    copies = 320
    vmem = lambda shape, dtype=BF16: pltpu.VMEM(shape, dtype)
    scratch = [
        vmem((width, ffw)), vmem((ffw, width)), vmem((width, hidden)), vmem((hidden, width)),
        vmem((nz, ny, tok, width + LANES)),
        vmem((nx, CORES, slots, width)),
        vmem((nx, CORES, slots, ffw), F32),
        vmem((nx, CORES, slots, ffw)),
        vmem((nx, CORES, slots, width)),
        vmem((nx, slots, width)),
        vmem((n_part, 2, nx // 2, slots, wide)),
        vmem((slots, width)),
        vmem((group, hidden)),
        vmem((hidden, group)), vmem((hidden, group), F32), vmem((hidden, group)),
        vmem((hidden, group), F32),
        vmem((nz, ny, tok, width)),
        vmem((ny, 2, nz // 2, tok, wide)),
        vmem((nz, 2, ny // 2, tok, wide)),
        vmem((2, nz // 2, tok, wide)),
        vmem((ny - 1, tok, wide)),
        vmem((nz, ny, tok, width)),
        vmem((2, nx, CORES, hidden, share)),
        vmem((2, nx, hidden, share)),
        vmem((2, 2, nx // 2, hidden, share)),
        pltpu.SemaphoreType.DMA((copies,)),
        pltpu.SemaphoreType.DMA((copies,)),
        pltpu.SemaphoreType.DMA((4,)),
    ]
    in_vmem = pl.BlockSpec(memory_space=pltpu.VMEM)
    anywhere = pl.BlockSpec(memory_space=pl.ANY)
    return pl.pallas_call(
        functools.partial(kernel, nz, ny, nx, scale, n_part),
        out_shape=(
            jax.ShapeDtypeStruct((share, hidden), F32),
            jax.ShapeDtypeStruct((hidden, share), F32),
        ),
        in_specs=[in_vmem] * 4 + [anywhere] * 4,
        out_specs=(in_vmem, in_vmem),
        scratch_shapes=scratch,
        cost_estimate=pl.CostEstimate(flops=15 * 10**9, bytes_accessed=11 * 10**6, transcendentals=0),
        compiler_params=pltpu.CompilerParams(
            collective_id=0, has_side_effects=True, vmem_limit_bytes=61 * 2**20
        ),
    )(tokens, expert_ids.T, gates.T, valid.reshape(1, tok), w_in, w_out, up_proj, down_proj)


def solution(mesh):
    n_expert, n_dp = mesh.shape["expert"], mesh.shape["dp"]
    ny = 4 if n_expert >= 16 else 2
    nz, nx = n_expert // ny, n_dp // CORES
    return jax.shard_map(
        functools.partial(per_device, nz, ny, nx),
        mesh=mesh,
        in_specs=(
            P(("dp", "expert"), None),
            P(("dp", "expert"), None),
            P(("dp", "expert"), None),
            P(("dp", "expert")),
            P("expert", None, "dp"),
            P("expert", "dp", None),
            P(None, "expert"),
            P("expert", None),
        ),
        out_specs=(P("dp", "expert"), P("expert", "dp")),
        check_vma=False,
    )
```

```python
import functools

import jax
import jax.numpy as jnp
from jax import lax
from jax.experimental import pallas as pl
from jax.experimental.pallas import tpu as pltpu
from jax.sharding import PartitionSpec as P

MESH = pl.DeviceIdType.MESH
CORES = 2
SLACK = 3.0
CAP = 4
PLANE_HOPS = (("z1", 1.0), ("z-1", 1.0), ("y1", 0.5), ("y-1", 0.5))
FOLD = 4
LANES = 128
Z_FIRST = 0
F32, BF16 = jnp.float32, jnp.bfloat16


def dot(a, b):
    return jnp.dot(a, b, preferred_element_type=F32)


def dot_nt(a, b):
    return lax.dot_general(a, b, (((1,), (1,)), ((), ())), preferred_element_type=F32)


class Event:
    def __init__(self):
        self.done = False


class Work:
    def __init__(self, us, rank=0):
        self.us, self.rank = us, rank


class Plan:
    RATE, INNER, LATENCY = 100e3, 400e3, 4.0

    def __init__(self):
        self.now, self.busy, self.processes = 0.0, {}, []

    def transfer(self, link, nbytes):
        if link == "plane":
            return max(self.transfer(way, nbytes * hops) for way, hops in PLANE_HOPS) + self.LATENCY
        start = max(self.now, self.busy.get(link, 0.0))
        self.busy[link] = start + nbytes / (self.INNER if link == "core" else self.RATE / CORES)
        return self.busy[link] + self.LATENCY

    def spawn(self, process):
        self.processes.append([process, self.now])

    def run(self):
        while self.processes:
            ready, works, later = [], [], []
            for i, (_, want) in enumerate(self.processes):
                if isinstance(want, Event):
                    if want.done:
                        ready.append((self.now, i))
                elif isinstance(want, Work):
                    works.append((want.rank, i))
                elif want <= self.now:
                    ready.append((want, i))
                else:
                    later.append((want, i))
            if ready:
                i = min(ready)[1]
            elif works:
                i = min(works)[1]
                self.now += self.processes[i][1].us
            else:
                self.now, i = min(later)
            process = self.processes[i]
            try:
                process[1] = next(process[0])
            except StopIteration:
                self.processes.remove(process)


def add_into(a, b):
    a[...] = (a[...].astype(F32) + b[...].astype(F32)).astype(BF16)


def kernel(
    nz, ny, nx, scale, n_part,
    tok_ref, ids_ref, gate_ref, valid_ref, win_hbm, wout_hbm, up_hbm, down_hbm,
    grad_ref,
    win, wout, up, down, grp, rows, acc, hid, part, part_in, xr, ret, got,
    hstu, hT, sgT, hgT, back, mix, zr, yr, zs, ys, og, gt, gt_in, gr,
    send_sem, recv_sem, load_sem,
):
    e, g = lax.axis_index("expert"), lax.axis_index("dp")
    z, y = e // ny, lax.rem(e, ny)
    x, c = g // CORES, lax.rem(g, CORES)
    tok, width = tok_ref.shape
    group = nz * ny * tok
    slots = nz * ny * CAP
    ffw = win.shape[1]
    wide = width // n_part
    share = width // (nx * CORES)

    def at_z(k):
        return (lax.rem(z + k, nz) * ny + y, g)

    def at_y(k):
        return (z * ny + lax.rem(y + k, ny), g)

    def at_x(k):
        return (e, lax.rem(x + k, nx) * CORES + c)

    sibling = (e, x * CORES + 1 - c)
    ring_z, ring_y, ring_x = (nz, z, at_z, "z"), (ny, y, at_y, "y"), (nx, x, at_x, "x")

    loads = [
        pltpu.make_async_copy(win_hbm.at[0], win, load_sem.at[0]),
        pltpu.make_async_copy(up_hbm, up, load_sem.at[1]),
        pltpu.make_async_copy(wout_hbm.at[0], wout, load_sem.at[2]),
        pltpu.make_async_copy(down_hbm, down, load_sem.at[3]),
    ]

    barrier = pltpu.get_barrier_semaphore()
    near = [sibling]
    near += [(lax.rem(e + k, nz * ny), g) for k in range(1, nz * ny)]
    near += [at_x(k) for k in sorted({1, nx - 1})]
    for device in near:
        pl.semaphore_signal(barrier, inc=1, device_id=device, device_id_type=MESH)
    for load in loads:
        load.start()

    row = lax.broadcasted_iota(jnp.int32, (LANES, tok), 0)
    expert, kind = row & 31, row >> 5
    first, second = ids_ref[0:1, :] == expert, ids_ref[1:2, :] == expert
    hot = jnp.where(first | second, 1.0, 0.0)
    before = lax.broadcasted_iota(jnp.int32, (tok, tok), 0) < lax.broadcasted_iota(jnp.int32, (tok, tok), 1)
    rank = dot(hot.astype(BF16), jnp.where(before, 1.0, 0.0).astype(BF16))
    gate = jnp.where(first, gate_ref[0:1, :], 0.0) + jnp.where(second, gate_ref[1:2, :], 0.0)
    high = gate.astype(BF16).astype(F32)
    table = jnp.where(kind == 0, hot * (1.0 + rank), jnp.where(kind == 1, high, gate - high))
    table = jnp.where(kind == 3, valid_ref[...].astype(F32), table)
    grp[z, y, :, 0:LANES] = table.T.astype(BF16)
    grp[z, y, :, LANES : LANES + width] = tok_ref[...]

    pl.semaphore_wait(barrier, len(near))

    plan = Plan()
    sent = []

    def send(src, dst, device, link):
        k = len(sent)
        copy = pltpu.make_async_remote_copy(
            src_ref=src, dst_ref=dst, send_sem=send_sem.at[k], recv_sem=recv_sem.at[k],
            device_id=device, device_id_type=MESH,
        )
        copy.start()
        size = 2
        for n in src.shape:
            size *= n
        sent.append(copy)
        return copy, plan.transfer(link, size)

    def ring_gather(ring, way, region, done, far, arrived=None):
        n, i, at, name = ring
        steps = n // 2 if way == far else n // 2 - 1
        for s in range(1, steps + 1):
            ref = region(lax.rem(i + n - way * (s - 1), n))
            copy, due = send(ref, ref, at(1 if way == 1 else n - 1), name + str(way))
            yield due
            copy.wait_recv()
            if arrived is not None:
                arrived(way * s)
        done.done = True

    def ring_sum(ring, way, own, landing, done, far, us, slack=0.0):
        n, i, at, name = ring
        steps = n // 2 if way == far else n // 2 - 1
        for s in range(1, steps + 1):
            place = lax.rem(i + n + way * (steps - s + 1), n)
            copy, due = send(own(place), landing(s - 1), at(1 if way == 1 else n - 1), name + str(way))
            yield due + slack
            copy.wait_recv()
            add_into(own(lax.rem(i + n + way * (steps - s), n)), landing(s - 1))
            plan.now += us
        done.done = True

    def both_ways(start):
        ends = []
        for way in (1, -1):
            ends.append(Event())
            plan.spawn(start(way, ends[-1]))
        return ends

    def all_of(events, done):
        for event in events:
            yield event
        done.done = True

    def y_then_z(buf, cols, done):
        ends = []

        def along_z(k):
            far = 1 if k in (0, 1) else -1
            region = lambda p: buf.at[p, lax.rem(y + ny - k, ny), :, cols]
            ends.extend(both_ways(lambda w, end: ring_gather(ring_z, w, region, end, far)))

        mine = buf.at[z, y, :, cols]
        hops = sorted(range(1, ny), key=lambda k: min(k, ny - k))
        copies = [(k, *send(mine, mine, at_y(k), "y1" if k <= ny // 2 else "y-1")) for k in hops]
        along_z(0)
        for k, copy, due in copies:
            yield due
            copy.wait_recv()
            along_z(k)
        plan.spawn(all_of(ends, done))

    def z_then_y(buf, cols, done):
        ends = []

        def along_y(k):
            far = 1 if len(ends) % 4 == 0 else -1
            region = lambda p: buf.at[lax.rem(z + nz - k, nz), p, :, cols]
            ends.extend(both_ways(lambda w, end: ring_gather(ring_y, w, region, end, far)))

        region = lambda p: buf.at[p, y, :, cols]
        firsts = both_ways(lambda w, end: ring_gather(ring_z, w, region, end, 1, along_y))
        along_y(0)
        for end in firsts:
            yield end
        plan.spawn(all_of(ends, done))

    def columns(q, shift):
        return pl.ds(q * wide + (shift if q else 0), wide + (0 if q else shift))

    def gather_plane(buf, q, shift, done):
        return (z_then_y if q == Z_FIRST else y_then_z)(buf, columns(q, shift), done)

    def sum_z_then_y(q, cols, done):
        from_y = []

        def along_z(k):
            to = lax.rem(y + k, ny)
            own = lambda p: mix.at[p, to, :, cols]
            landing = lambda w: lambda s: zr.at[k, (1 - w) // 2, s]
            far = 1 if k in (0, 1) else -1
            for end in both_ways(lambda w, end: ring_sum(ring_z, w, own, landing(w), end, far, 0.1, SLACK)):
                yield end
            if k:
                from_y.append(
                    send(mix.at[z, to, :, cols], ys.at[k - 1], at_y(k), "y1" if k <= ny // 2 else "y-1")
                )
            finished[k].done = True

        finished = [Event() for _ in range(ny)]
        for k in sorted(range(ny), key=lambda k: -min(k, ny - k)):
            plan.spawn(along_z(k))
        for event in finished:
            yield event
        for copy, due in from_y:
            yield due
            copy.wait_recv()
        done.done = True

    def sum_y_then_z(q, cols, done):
        finished = [Event() for _ in range(nz)]

        def along_y(k, far):
            to = lax.rem(z + k, nz)
            own = lambda p: mix.at[to, p, :, cols]
            landing = lambda w: lambda s: yr.at[k, (1 - w) // 2, s]
            for end in both_ways(lambda w, end: ring_sum(ring_y, w, own, landing(w), end, far, 0.1, SLACK)):
                yield end
            finished[k].done = True

        def along_z(way, end):
            n, i, at, name = ring_z
            steps = n // 2 if way == 1 else n // 2 - 1
            for s in range(1, steps + 1):
                k = steps - s + 1
                yield finished[(way * k) % n]
                copy, due = send(
                    mix.at[lax.rem(i + n + way * k, n), y, :, cols], zs.at[(1 - way) // 2, s - 1],
                    at(1 if way == 1 else n - 1), name + str(way),
                )
                yield due + SLACK
                copy.wait_recv()
                yield finished[(way * (k - 1)) % n]
                add_into(mix.at[lax.rem(i + n + way * (k - 1), n), y, :, cols], zs.at[(1 - way) // 2, s - 1])
                plan.now += 0.1
            end.done = True

        for at, k in enumerate(sorted(range(nz), key=lambda k: -min(k, nz - k))):
            plan.spawn(along_y(k, 1 if at % 2 == 0 else -1))
        for end in both_ways(along_z):
            yield end
        done.done = True

    each = lambda: [Event() for _ in range(n_part)]
    gathered, selected, hidden, summed, mixed, out, grads = each(), each(), each(), each(), each(), each(), each()
    student = Event()
    part_cols = lambda q: pl.ds(q * wide, wide)
    hops = nx // 2
    order = [nx // 2] + [k for k in range(1, nx) if k != nx // 2] + [0]
    whole = [[Event() for _ in range(nx)] for _ in range(n_part)]
    multiplied = [[Event() for _ in range(nx)] for _ in range(n_part)]

    def take_slots(q):
        if q:
            yield selected[q - 1]
        yield gathered[q]
        pick = jnp.where(lax.broadcasted_iota(jnp.int32, (16, LANES), 1) == e, 1.0, 0.0).astype(BF16)
        ranks_row = dot_nt(pick, grp[:, :, :, 0:LANES].reshape(group, LANES))[0:1, :]
        slot = lax.broadcasted_iota(jnp.int32, (slots, group), 0)
        token = lax.broadcasted_iota(jnp.int32, (slots, group), 1)
        chosen = (slot // CAP == token // tok) & (ranks_row == ((slot & (CAP - 1)) + 1).astype(F32))
        select = jnp.where(chosen, 1.0, 0.0).astype(BF16)
        tile = min(512, wide)
        for j in range(wide // tile):
            at = q * wide + j * tile
            block = grp[:, :, :, LANES + at : LANES + at + tile].reshape(group, tile)
            rows[x, c, :, at : at + tile] = dot(select, block).astype(BF16)
        plan.now += 0.6
        selected[q].done = True
        cols = part_cols(q)
        fromsib = {k: [] for k in range(nx)}
        low, high = pl.ds(0, slots // 2), pl.ds(slots // 2, slots // 2)

        def to_sibling(k, p, where):
            ref = rows.at[p, c, where, cols]
            fromsib[k].append(send(ref, ref, sibling, "core"))
            if len(fromsib[k]) == (2 if k else 1):
                plan.spawn(settle(k))

        def settle(k):
            for copy, due in fromsib[k]:
                yield due
                copy.wait_recv()
            whole[q][k].done = True

        to_sibling(0, x, pl.ds(0, slots))
        for where, far in ((low, 1), (high, -1)):
            region = lambda p, where=where: rows.at[p, c, where, cols]
            both_ways(
                lambda w, end, where=where, region=region, far=far: ring_gather(
                    ring_x, w, region, end, far,
                    lambda d, where=where: to_sibling(d % nx, lax.rem(x + nx - d, nx), where),
                )
            )

    def place_of(k):
        return lax.rem(x + nx - k, nx)

    def first_product(q):
        for k in [0] + [k for k in range(1, nx) if k != hops] + [hops]:
            yield whole[q][k]
            if q:
                yield multiplied[q - 1][k]
            yield Work(1.4)
            if q == 0 and k == 0:
                loads[0].wait()
            p = place_of(k)
            tile = min(256, ffw)

            @pl.loop(0, ffw // tile)
            def _(j):
                cols = pl.ds(pl.multiple_of(j * tile, tile), tile)
                value = dot(
                    rows[p, :, :, part_cols(q)].reshape(CORES * slots, wide), win[part_cols(q), cols]
                ).reshape(CORES, slots, tile)
                if q:
                    value = value + acc[p, :, :, cols]
                if q < n_part - 1:
                    acc[p, :, :, cols] = value
                else:
                    hid[p, :, :, cols] = jnp.maximum(value, 0.0).astype(BF16)

            multiplied[q][k].done = True
        hidden[q].done = True

    def second_product(q):
        yield hidden[n_part - 1]
        if q:
            yield Work(0.0, q)
        if q == 0:
            loads[2].wait()
        tile = min(256, wide)
        for j in range(wide // tile):
            yield Work(1.0, q)
            cols = pl.ds(q * wide + j * tile, tile)
            value = dot(hid[...].reshape(nx * CORES * slots, ffw), wout[:, cols])
            part[:, :, :, cols] = value.astype(BF16).reshape(nx, CORES, slots, tile)
        cols = part_cols(q)
        swaps = []
        for k in order:
            p = lax.rem(x + k, nx)
            swaps.append(send(part.at[p, 1 - c, :, cols], part_in.at[p, :, cols], sibling, "core"))
        for k, (copy, due) in zip(order, swaps):
            p = lax.rem(x + k, nx)
            yield due
            copy.wait_recv()
            add_into(part.at[p, c, :, cols], part_in.at[p, :, cols])
        ends = []
        for h, far in ((0, 1), (1, -1)):
            where = pl.ds(h * (slots // 2), slots // 2)
            own = lambda p, where=where: part.at[p, c, where, cols]
            landing = lambda w, where=where: lambda s: xr.at[q, (1 - w) // 2, s, where]
            ends += both_ways(
                lambda w, end, own=own, landing=landing, far=far: ring_sum(
                    ring_x, w, own, landing(w), end, far, 0.15
                )
            )
        for end in ends:
            yield end
        n_place, fold = nz * ny, wide // FOLD
        i = lax.broadcasted_iota(jnp.int32, (n_place * CAP * FOLD, slots), 0)
        slot = lax.broadcasted_iota(jnp.int32, (n_place * CAP * FOLD, slots), 1)
        at_row = slot == (i >> 4) * CAP + (i & 3)
        folded = jnp.zeros((n_place * CAP * FOLD, fold), F32)
        for f in range(FOLD):
            move = jnp.where(at_row & (((i >> 2) & 3) == f), 1.0, 0.0).astype(BF16)
            folded = folded + dot(move, part[x, c, :, q * wide + f * fold : q * wide + (f + 1) * fold])
        ret[q] = folded.astype(BF16).reshape(n_place, CAP * FOLD, fold)
        got[q, e] = ret[q, e]
        plan.now += 0.8
        backs = []
        for k in range(1, n_place):
            to = lax.rem(e + k, n_place)
            backs.append(send(ret.at[q, to], got.at[q, e], (to, g), "plane"))
        for copy, due in backs:
            yield due
            copy.wait_recv()
        summed[q].done = True

    blocks = 2 if nz % 2 == 0 else 1
    step = blocks * ny * tok

    def student_forward():
        for event in gathered:
            yield event
        loads[1].wait()
        for k in range(group // step):
            yield Work(1.0, 5)
            at = k * step
            block = grp[k * blocks : (k + 1) * blocks, :, :, LANES : LANES + width].reshape(step, width)
            value = dot(block, up[...])
            sig = jax.nn.sigmoid(value)
            act = value * sig
            hstu[at : at + step, :] = act.astype(BF16)
            hT[:, at : at + step] = act.T.astype(BF16)
            sgT[:, at : at + step] = (sig * (1.0 + value * (1.0 - sig))).T
        student.done = True

    def student_output(q):
        yield student
        yield Work(1.2, 6)
        if q == 0:
            loads[3].wait()
        tile = min(512, wide)

        @pl.loop(0, group // step)
        def _(k):
            at = pl.multiple_of(k * step, step)
            for j in range(wide // tile):
                cols = slice(q * wide + j * tile, q * wide + (j + 1) * tile)
                value = dot(hstu[pl.ds(at, step), :], down[:, cols])
                mix[pl.ds(k * blocks, blocks), :, :, cols] = value.astype(BF16).reshape(blocks, ny, tok, tile)

        plan.spawn((sum_y_then_z if q == Z_FIRST else sum_z_then_y)(q, columns(q, 0), mixed[q]))

    def output_grad(q):
        yield mixed[q]
        yield summed[q]
        cols = columns(q, 0)
        value = mix[z, y, :, cols].astype(F32)
        if q != Z_FIRST:
            for k in range(ny - 1):
                value = value + ys[k].astype(F32)
        n_row = nz * ny * CAP * FOLD
        table = grp[z, y, :, 0:LANES]
        line = lax.broadcasted_iota(jnp.int32, (LANES, n_row), 0)
        source = lax.broadcasted_iota(jnp.int32, (LANES, n_row), 1) >> 4
        spread = lambda off: dot(table, jnp.where(line == source + off, 1.0, 0.0).astype(BF16))
        ranks, high, low = spread(0), spread(32), spread(64)
        i = lax.broadcasted_iota(jnp.int32, (tok, n_row), 1)
        named = ranks == ((i & 3) + 1).astype(F32)
        back_rows = got[q].reshape(n_row, wide // FOLD)
        pieces = []
        for f in range(FOLD):
            here = named & (((i >> 2) & 3) == f)
            pieces.append(
                dot(jnp.where(here, high, 0.0).astype(BF16), back_rows)
                + dot(jnp.where(here, low, 0.0).astype(BF16), back_rows)
            )
        value = value - jnp.concatenate(pieces, axis=1)
        og[z, y, :, cols] = (grp[z, y, :, 96:97].astype(F32) * scale * value).astype(BF16)
        plan.now += 0.8
        plan.spawn(gather_plane(og, q, 0, grads[q]))

    def to_places(kind):
        swap, due = send(gt.at[kind, :, 1 - c], gt_in.at[kind], sibling, "core")
        yield due
        swap.wait_recv()
        for p in range(nx):
            add_into(gt.at[kind, p, c], gt_in.at[kind, p])
        n = gt.shape[3]
        ends = []
        for h, far in ((0, 1), (1, -1)):
            where = pl.ds(h * (n // 2), n // 2)
            own = lambda p, where=where: gt.at[kind, p, c, where]
            landing = lambda w, where=where: lambda s: gr.at[kind, (1 - w) // 2, s, where]
            ends += both_ways(
                lambda w, end, own=own, landing=landing, far=far: ring_sum(
                    ring_x, w, own, landing(w), end, far, 0.05
                )
            )
        for end in ends:
            yield end
        if kind:
            grad_ref[1] = gt[1, x, c]
        else:
            grad_ref[0] = gt[0, x, c].astype(F32).T.astype(BF16)

    def backward():
        per_part = nx * CORES // n_part
        for q in range(n_part):
            yield grads[q]
            yield Work(1.2)

            @pl.loop(0, per_part)
            def _(k):
                to = q * per_part + k
                cols = pl.ds(pl.multiple_of(to * share, share), share)
                value = dot(hT[...], og[:, :, :, cols].reshape(group, share))
                gt[1, to // CORES, lax.rem(to, CORES)] = value.astype(BF16)

            if q == n_part - 1:
                plan.spawn(to_places(1))
            yield Work(1.2)

            @pl.loop(0, group // step)
            def _(k):
                block = og[pl.ds(k * blocks, blocks), :, :, part_cols(q)].reshape(step, wide)
                place = pl.ds(pl.multiple_of(k * step, step), step)
                value = dot_nt(down[:, part_cols(q)], block)
                if q:
                    value = value + back[:, place]
                if q < n_part - 1:
                    back[:, place] = value
                else:
                    hgT[:, place] = (value * sgT[:, place]).astype(BF16)

        yield Work(2.2)

        @pl.loop(0, nx * CORES)
        def _(k):
            cols = pl.ds(pl.multiple_of(LANES + k * share, LANES), share)
            value = dot(hgT[...], grp[:, :, :, cols].reshape(group, share))
            gt[0, k // CORES, lax.rem(k, CORES)] = value.astype(BF16)

        plan.spawn(to_places(0))

    for q in range(n_part):
        plan.spawn(gather_plane(grp, q, LANES, gathered[q]))
        plan.spawn(take_slots(q))
        plan.spawn(first_product(q))
        plan.spawn(second_product(q))
        plan.spawn(student_output(q))
        plan.spawn(output_grad(q))
    plan.spawn(student_forward())
    plan.spawn(backward())
    plan.run()

    for copy in sent:
        copy.wait_send()


def per_device(nz, ny, nx, tokens, expert_ids, gates, valid, w_in, w_out, up_proj, down_proj):
    tok, width = tokens.shape
    ffw, hidden = w_in.shape[2], up_proj.shape[1]
    group = nz * ny * tok
    slots = nz * ny * CAP
    share = width // (nx * CORES)
    scale = 1.0 / float(group * nx * CORES) ** 0.5
    n_part = 2
    wide = width // n_part
    copies = 384
    vmem = lambda shape, dtype=BF16: pltpu.VMEM(shape, dtype)
    scratch = [
        vmem((width, ffw)), vmem((ffw, width)), vmem((width, hidden)), vmem((hidden, width)),
        vmem((nz, ny, tok, width + LANES)),
        vmem((nx, CORES, slots, width)),
        vmem((nx, CORES, slots, ffw), F32),
        vmem((nx, CORES, slots, ffw)),
        vmem((nx, CORES, slots, width)),
        vmem((nx, slots, width)),
        vmem((n_part, 2, nx // 2, slots, wide)),
        vmem((n_part, nz * ny, CAP * FOLD, wide // FOLD)),
        vmem((n_part, nz * ny, CAP * FOLD, wide // FOLD)),
        vmem((group, hidden)),
        vmem((hidden, group)), vmem((hidden, group), F32), vmem((hidden, group)),
        vmem((hidden, group), F32),
        vmem((nz, ny, tok, width)),
        vmem((ny, 2, nz // 2, tok, wide)),
        vmem((nz, 2, ny // 2, tok, wide)),
        vmem((2, nz // 2, tok, wide)),
        vmem((ny - 1, tok, wide)),
        vmem((nz, ny, tok, width)),
        vmem((2, nx, CORES, hidden, share)),
        vmem((2, nx, hidden, share)),
        vmem((2, 2, nx // 2, hidden, share)),
        pltpu.SemaphoreType.DMA((copies,)),
        pltpu.SemaphoreType.DMA((copies,)),
        pltpu.SemaphoreType.DMA((4,)),
    ]
    in_vmem = pl.BlockSpec(memory_space=pltpu.VMEM)
    anywhere = pl.BlockSpec(memory_space=pl.ANY)
    grads = pl.pallas_call(
        functools.partial(kernel, nz, ny, nx, scale, n_part),
        out_shape=jax.ShapeDtypeStruct((2, share, hidden), BF16),
        in_specs=[in_vmem] * 4 + [anywhere] * 4,
        out_specs=in_vmem,
        scratch_shapes=scratch,
        cost_estimate=pl.CostEstimate(flops=15 * 10**9, bytes_accessed=11 * 10**6, transcendentals=0),
        compiler_params=pltpu.CompilerParams(
            collective_id=0, has_side_effects=True, vmem_limit_bytes=61 * 2**20
        ),
    )(tokens, expert_ids.T, gates.T, valid.reshape(1, tok), w_in, w_out, up_proj, down_proj)
    return grads[0].astype(F32), grads[1].reshape(hidden, share).astype(F32)


def solution(mesh):
    n_expert, n_dp = mesh.shape["expert"], mesh.shape["dp"]
    ny = 4 if n_expert >= 16 else 2
    nz, nx = n_expert // ny, n_dp // CORES
    return jax.shard_map(
        functools.partial(per_device, nz, ny, nx),
        mesh=mesh,
        in_specs=(
            P(("dp", "expert"), None),
            P(("dp", "expert"), None),
            P(("dp", "expert"), None),
            P(("dp", "expert")),
            P("expert", None, "dp"),
            P("expert", "dp", None),
            P(None, "expert"),
            P("expert", None),
        ),
        out_specs=(P("dp", "expert"), P("expert", "dp")),
        check_vma=False,
    )
```

```python
import functools

import jax
import jax.numpy as jnp
from jax import lax
from jax.experimental import pallas as pl
from jax.experimental.pallas import tpu as pltpu
from jax.sharding import PartitionSpec as P

MESH = pl.DeviceIdType.MESH
CORES = 2
SLACK = 6.0
CAP = 4
PLANE_HOPS = (("z1", 1.0), ("z-1", 1.0), ("y1", 0.5), ("y-1", 0.5))
FOLD = 4
LANES = 128
Z_FIRST = 0
F32, BF16 = jnp.float32, jnp.bfloat16


def dot(a, b):
    return jnp.dot(a, b, preferred_element_type=F32)


def dot_nt(a, b):
    return lax.dot_general(a, b, (((1,), (1,)), ((), ())), preferred_element_type=F32)


class Event:
    def __init__(self):
        self.done = False


class Work:
    def __init__(self, us, rank=0):
        self.us, self.rank = us, rank


class Plan:
    RATE, INNER, LATENCY = 100e3, 400e3, 4.0

    def __init__(self):
        self.now, self.busy, self.processes = 0.0, {}, []

    def transfer(self, link, nbytes):
        if link == "plane":
            return max(self.transfer(way, nbytes * hops) for way, hops in PLANE_HOPS) + self.LATENCY
        start = max(self.now, self.busy.get(link, 0.0))
        self.busy[link] = start + nbytes / (self.INNER if link == "core" else self.RATE / CORES)
        return self.busy[link] + self.LATENCY

    def spawn(self, process):
        self.processes.append([process, self.now])

    def run(self):
        while self.processes:
            ready, works, later = [], [], []
            for i, (_, want) in enumerate(self.processes):
                if isinstance(want, Event):
                    if want.done:
                        ready.append((self.now, i))
                elif isinstance(want, Work):
                    works.append((want.rank, i))
                elif want <= self.now:
                    ready.append((want, i))
                else:
                    later.append((want, i))
            if ready:
                i = min(ready)[1]
            elif works:
                i = min(works)[1]
                self.now += self.processes[i][1].us
            else:
                self.now, i = min(later)
            process = self.processes[i]
            try:
                process[1] = next(process[0])
            except StopIteration:
                self.processes.remove(process)


def add_into(a, b):
    a[...] = (a[...].astype(F32) + b[...].astype(F32)).astype(BF16)


def kernel(
    nz, ny, nx, scale, n_part,
    tok_ref, ids_ref, gate_ref, valid_ref, win_hbm, wout_hbm, up_hbm, down_hbm,
    grad_ref,
    win, wout, up, down, grp, rows, acc, hid, part, part_in, xr, ret, got,
    hstu, hT, sgT, hgT, back, mix, zr, yr, zs, ys, og, gt, gt_in, gr,
    send_sem, recv_sem, load_sem,
):
    e, g = lax.axis_index("expert"), lax.axis_index("dp")
    z, y = e // ny, lax.rem(e, ny)
    x, c = g // CORES, lax.rem(g, CORES)
    tok, width = tok_ref.shape
    group = nz * ny * tok
    slots = nz * ny * CAP
    ffw = win.shape[1]
    wide = width // n_part
    share = width // (nx * CORES)

    def at_z(k):
        return (lax.rem(z + k, nz) * ny + y, g)

    def at_y(k):
        return (z * ny + lax.rem(y + k, ny), g)

    def at_x(k):
        return (e, lax.rem(x + k, nx) * CORES + c)

    sibling = (e, x * CORES + 1 - c)
    ring_z, ring_y, ring_x = (nz, z, at_z, "z"), (ny, y, at_y, "y"), (nx, x, at_x, "x")

    loads = [
        pltpu.make_async_copy(win_hbm.at[0], win, load_sem.at[0]),
        pltpu.make_async_copy(up_hbm, up, load_sem.at[1]),
        pltpu.make_async_copy(wout_hbm.at[0], wout, load_sem.at[2]),
        pltpu.make_async_copy(down_hbm, down, load_sem.at[3]),
    ]

    barrier = pltpu.get_barrier_semaphore()
    near = [sibling]
    near += [(lax.rem(e + k, nz * ny), g) for k in range(1, nz * ny)]
    near += [at_x(k) for k in sorted({1, nx - 1})]
    for device in near:
        pl.semaphore_signal(barrier, inc=1, device_id=device, device_id_type=MESH)
    for load in loads:
        load.start()

    row = lax.broadcasted_iota(jnp.int32, (LANES, tok), 0)
    expert, kind = row & 31, row >> 5
    first, second = ids_ref[0:1, :] == expert, ids_ref[1:2, :] == expert
    hot = jnp.where(first | second, 1.0, 0.0)
    before = lax.broadcasted_iota(jnp.int32, (tok, tok), 0) < lax.broadcasted_iota(jnp.int32, (tok, tok), 1)
    rank = dot(hot.astype(BF16), jnp.where(before, 1.0, 0.0).astype(BF16))
    gate = jnp.where(first, gate_ref[0:1, :], 0.0) + jnp.where(second, gate_ref[1:2, :], 0.0)
    high = gate.astype(BF16).astype(F32)
    table = jnp.where(kind == 0, hot * (1.0 + rank), jnp.where(kind == 1, high, gate - high))
    table = jnp.where(kind == 3, valid_ref[...].astype(F32), table)
    grp[z, y, :, 0:LANES] = table.T.astype(BF16)
    grp[z, y, :, LANES : LANES + width] = tok_ref[...]

    pl.semaphore_wait(barrier, len(near))

    plan = Plan()
    sent = []

    def send(src, dst, device, link):
        k = len(sent)
        copy = pltpu.make_async_remote_copy(
            src_ref=src, dst_ref=dst, send_sem=send_sem.at[k], recv_sem=recv_sem.at[k],
            device_id=device, device_id_type=MESH,
        )
        copy.start()
        size = 2
        for n in src.shape:
            size *= n
        sent.append(copy)
        return copy, plan.transfer(link, size)

    def ring_gather(ring, way, region, done, far, arrived=None):
        n, i, at, name = ring
        steps = n // 2 if way == far else n // 2 - 1
        for s in range(1, steps + 1):
            ref = region(lax.rem(i + n - way * (s - 1), n))
            copy, due = send(ref, ref, at(1 if way == 1 else n - 1), name + str(way))
            yield due
            copy.wait_recv()
            if arrived is not None:
                arrived(way * s)
        done.done = True

    def ring_sum(ring, way, own, landing, done, far, us, slack=0.0):
        n, i, at, name = ring
        steps = n // 2 if way == far else n // 2 - 1
        for s in range(1, steps + 1):
            place = lax.rem(i + n + way * (steps - s + 1), n)
            copy, due = send(own(place), landing(s - 1), at(1 if way == 1 else n - 1), name + str(way))
            yield due + slack
            copy.wait_recv()
            add_into(own(lax.rem(i + n + way * (steps - s), n)), landing(s - 1))
            plan.now += us
        done.done = True

    def both_ways(start):
        ends = []
        for way in (1, -1):
            ends.append(Event())
            plan.spawn(start(way, ends[-1]))
        return ends

    def all_of(events, done):
        for event in events:
            yield event
        done.done = True

    def y_then_z(buf, cols, done):
        ends = []

        def along_z(k):
            far = 1 if k in (0, 1) else -1
            region = lambda p: buf.at[p, lax.rem(y + ny - k, ny), :, cols]
            ends.extend(both_ways(lambda w, end: ring_gather(ring_z, w, region, end, far)))

        mine = buf.at[z, y, :, cols]
        hops = sorted(range(1, ny), key=lambda k: min(k, ny - k))
        copies = [(k, *send(mine, mine, at_y(k), "y1" if k <= ny // 2 else "y-1")) for k in hops]
        along_z(0)
        for k, copy, due in copies:
            yield due
            copy.wait_recv()
            along_z(k)
        plan.spawn(all_of(ends, done))

    def z_then_y(buf, cols, done):
        ends = []

        def along_y(k):
            far = 1 if len(ends) % 4 == 0 else -1
            region = lambda p: buf.at[lax.rem(z + nz - k, nz), p, :, cols]
            ends.extend(both_ways(lambda w, end: ring_gather(ring_y, w, region, end, far)))

        region = lambda p: buf.at[p, y, :, cols]
        firsts = both_ways(lambda w, end: ring_gather(ring_z, w, region, end, 1, along_y))
        along_y(0)
        for end in firsts:
            yield end
        plan.spawn(all_of(ends, done))

    def columns(q, shift):
        return pl.ds(q * wide + (shift if q else 0), wide + (0 if q else shift))

    def gather_plane(buf, q, shift, done):
        return (z_then_y if q == Z_FIRST else y_then_z)(buf, columns(q, shift), done)

    def sum_z_then_y(q, cols, done):
        from_y = []

        def along_z(k):
            to = lax.rem(y + k, ny)
            own = lambda p: mix.at[p, to, :, cols]
            landing = lambda w: lambda s: zr.at[k, (1 - w) // 2, s]
            far = 1 if k in (0, 1) else -1
            for end in both_ways(lambda w, end: ring_sum(ring_z, w, own, landing(w), end, far, 0.1, SLACK)):
                yield end
            if k:
                from_y.append(
                    send(mix.at[z, to, :, cols], ys.at[k - 1], at_y(k), "y1" if k <= ny // 2 else "y-1")
                )
            finished[k].done = True

        finished = [Event() for _ in range(ny)]
        for k in sorted(range(ny), key=lambda k: -min(k, ny - k)):
            plan.spawn(along_z(k))
        for event in finished:
            yield event
        for copy, due in from_y:
            yield due
            copy.wait_recv()
        done.done = True

    def sum_y_then_z(q, cols, done):
        finished = [Event() for _ in range(nz)]

        def along_y(k, far):
            to = lax.rem(z + k, nz)
            own = lambda p: mix.at[to, p, :, cols]
            landing = lambda w: lambda s: yr.at[k, (1 - w) // 2, s]
            for end in both_ways(lambda w, end: ring_sum(ring_y, w, own, landing(w), end, far, 0.1, SLACK)):
                yield end
            finished[k].done = True

        def along_z(way, end):
            n, i, at, name = ring_z
            steps = n // 2 if way == 1 else n // 2 - 1
            for s in range(1, steps + 1):
                k = steps - s + 1
                yield finished[(way * k) % n]
                copy, due = send(
                    mix.at[lax.rem(i + n + way * k, n), y, :, cols], zs.at[(1 - way) // 2, s - 1],
                    at(1 if way == 1 else n - 1), name + str(way),
                )
                yield due + SLACK
                copy.wait_recv()
                yield finished[(way * (k - 1)) % n]
                add_into(mix.at[lax.rem(i + n + way * (k - 1), n), y, :, cols], zs.at[(1 - way) // 2, s - 1])
                plan.now += 0.1
            end.done = True

        for at, k in enumerate(sorted(range(nz), key=lambda k: -min(k, nz - k))):
            plan.spawn(along_y(k, 1 if at % 2 == 0 else -1))
        for end in both_ways(along_z):
            yield end
        done.done = True

    each = lambda: [Event() for _ in range(n_part)]
    gathered, selected, hidden, summed, mixed, out, grads = each(), each(), each(), each(), each(), each(), each()
    student = Event()
    part_cols = lambda q: pl.ds(q * wide, wide)
    hops = nx // 2
    order = [nx // 2] + [k for k in range(1, nx) if k != nx // 2] + [0]
    whole = [[Event() for _ in range(nx)] for _ in range(n_part)]
    multiplied = [[Event() for _ in range(nx)] for _ in range(n_part)]

    def take_slots(q):
        if q:
            yield selected[q - 1]
        yield gathered[q]
        pick = jnp.where(lax.broadcasted_iota(jnp.int32, (16, LANES), 1) == e, 1.0, 0.0).astype(BF16)
        ranks_row = dot_nt(pick, grp[:, :, :, 0:LANES].reshape(group, LANES))[0:1, :]
        slot = lax.broadcasted_iota(jnp.int32, (slots, group), 0)
        token = lax.broadcasted_iota(jnp.int32, (slots, group), 1)
        chosen = (slot // CAP == token // tok) & (ranks_row == ((slot & (CAP - 1)) + 1).astype(F32))
        select = jnp.where(chosen, 1.0, 0.0).astype(BF16)
        tile = min(512, wide)
        for j in range(wide // tile):
            at = q * wide + j * tile
            block = grp[:, :, :, LANES + at : LANES + at + tile].reshape(group, tile)
            rows[x, c, :, at : at + tile] = dot(select, block).astype(BF16)
        plan.now += 0.6
        selected[q].done = True
        cols = part_cols(q)
        fromsib = {k: [] for k in range(nx)}
        low, high = pl.ds(0, slots // 2), pl.ds(slots // 2, slots // 2)

        def to_sibling(k, p, where):
            ref = rows.at[p, c, where, cols]
            fromsib[k].append(send(ref, ref, sibling, "core"))
            if len(fromsib[k]) == (2 if k else 1):
                plan.spawn(settle(k))

        def settle(k):
            for copy, due in fromsib[k]:
                yield due
                copy.wait_recv()
            whole[q][k].done = True

        to_sibling(0, x, pl.ds(0, slots))
        for where, far in ((low, 1), (high, -1)):
            region = lambda p, where=where: rows.at[p, c, where, cols]
            both_ways(
                lambda w, end, where=where, region=region, far=far: ring_gather(
                    ring_x, w, region, end, far,
                    lambda d, where=where: to_sibling(d % nx, lax.rem(x + nx - d, nx), where),
                )
            )

    def place_of(k):
        return lax.rem(x + nx - k, nx)

    def first_product(q):
        for k in [0] + [k for k in range(1, nx) if k != hops] + [hops]:
            yield whole[q][k]
            if q:
                yield multiplied[q - 1][k]
            yield Work(1.4)
            if q == 0 and k == 0:
                loads[0].wait()
            p = place_of(k)
            tile = min(256, ffw)

            @pl.loop(0, ffw // tile)
            def _(j):
                cols = pl.ds(pl.multiple_of(j * tile, tile), tile)
                value = dot(
                    rows[p, :, :, part_cols(q)].reshape(CORES * slots, wide), win[part_cols(q), cols]
                ).reshape(CORES, slots, tile)
                if q:
                    value = value + acc[p, :, :, cols]
                if q < n_part - 1:
                    acc[p, :, :, cols] = value
                else:
                    hid[p, :, :, cols] = jnp.maximum(value, 0.0).astype(BF16)

            multiplied[q][k].done = True
        hidden[q].done = True

    def second_product(q):
        yield hidden[n_part - 1]
        if q:
            yield Work(0.0, q)
        if q == 0:
            loads[2].wait()
        tile = min(256, wide)
        for j in range(wide // tile):
            yield Work(1.0, q)
            cols = pl.ds(q * wide + j * tile, tile)
            value = dot(hid[...].reshape(nx * CORES * slots, ffw), wout[:, cols])
            part[:, :, :, cols] = value.astype(BF16).reshape(nx, CORES, slots, tile)
        cols = part_cols(q)
        swaps = []
        for k in order:
            p = lax.rem(x + k, nx)
            swaps.append(send(part.at[p, 1 - c, :, cols], part_in.at[p, :, cols], sibling, "core"))
        for k, (copy, due) in zip(order, swaps):
            p = lax.rem(x + k, nx)
            yield due
            copy.wait_recv()
            add_into(part.at[p, c, :, cols], part_in.at[p, :, cols])
        ends = []
        for h, far in ((0, 1), (1, -1)):
            where = pl.ds(h * (slots // 2), slots // 2)
            own = lambda p, where=where: part.at[p, c, where, cols]
            landing = lambda w, where=where: lambda s: xr.at[q, (1 - w) // 2, s, where]
            ends += both_ways(
                lambda w, end, own=own, landing=landing, far=far: ring_sum(
                    ring_x, w, own, landing(w), end, far, 0.15
                )
            )
        for end in ends:
            yield end
        n_place, fold = nz * ny, wide // FOLD
        i = lax.broadcasted_iota(jnp.int32, (n_place * CAP * FOLD, slots), 0)
        slot = lax.broadcasted_iota(jnp.int32, (n_place * CAP * FOLD, slots), 1)
        at_row = slot == (i >> 4) * CAP + (i & 3)
        folded = jnp.zeros((n_place * CAP * FOLD, fold), F32)
        for f in range(FOLD):
            move = jnp.where(at_row & (((i >> 2) & 3) == f), 1.0, 0.0).astype(BF16)
            folded = folded + dot(move, part[x, c, :, q * wide + f * fold : q * wide + (f + 1) * fold])
        ret[q] = folded.astype(BF16).reshape(n_place, CAP * FOLD, fold)
        got[q, e] = ret[q, e]
        plan.now += 0.8
        backs = []
        for k in range(1, n_place):
            to = lax.rem(e + k, n_place)
            backs.append(send(ret.at[q, to], got.at[q, e], (to, g), "plane"))
        for copy, due in backs:
            yield due
            copy.wait_recv()
        summed[q].done = True

    blocks = 2 if nz % 2 == 0 else 1
    step = blocks * ny * tok

    def student_forward():
        for event in gathered:
            yield event
        loads[1].wait()
        for k in range(group // step):
            yield Work(1.0, 5)
            at = k * step
            block = grp[k * blocks : (k + 1) * blocks, :, :, LANES : LANES + width].reshape(step, width)
            value = dot(block, up[...])
            sig = jax.nn.sigmoid(value)
            act = value * sig
            hstu[at : at + step, :] = act.astype(BF16)
            hT[:, at : at + step] = act.T.astype(BF16)
            sgT[:, at : at + step] = (sig * (1.0 + value * (1.0 - sig))).T
        student.done = True

    def student_output(q):
        yield student
        yield Work(1.2, 6)
        if q == 0:
            loads[3].wait()
        tile = min(512, wide)

        @pl.loop(0, group // step)
        def _(k):
            at = pl.multiple_of(k * step, step)
            for j in range(wide // tile):
                cols = slice(q * wide + j * tile, q * wide + (j + 1) * tile)
                value = dot(hstu[pl.ds(at, step), :], down[:, cols])
                mix[pl.ds(k * blocks, blocks), :, :, cols] = value.astype(BF16).reshape(blocks, ny, tok, tile)

        plan.spawn((sum_y_then_z if q == Z_FIRST else sum_z_then_y)(q, columns(q, 0), mixed[q]))

    def output_grad(q):
        yield mixed[q]
        yield summed[q]
        cols = columns(q, 0)
        value = mix[z, y, :, cols].astype(F32)
        if q != Z_FIRST:
            for k in range(ny - 1):
                value = value + ys[k].astype(F32)
        n_row = nz * ny * CAP * FOLD
        table = grp[z, y, :, 0:LANES]
        line = lax.broadcasted_iota(jnp.int32, (LANES, n_row), 0)
        source = lax.broadcasted_iota(jnp.int32, (LANES, n_row), 1) >> 4
        spread = lambda off: dot(table, jnp.where(line == source + off, 1.0, 0.0).astype(BF16))
        ranks, high, low = spread(0), spread(32), spread(64)
        i = lax.broadcasted_iota(jnp.int32, (tok, n_row), 1)
        named = ranks == ((i & 3) + 1).astype(F32)
        back_rows = got[q].reshape(n_row, wide // FOLD)
        pieces = []
        for f in range(FOLD):
            here = named & (((i >> 2) & 3) == f)
            pieces.append(
                dot(jnp.where(here, high, 0.0).astype(BF16), back_rows)
                + dot(jnp.where(here, low, 0.0).astype(BF16), back_rows)
            )
        value = value - jnp.concatenate(pieces, axis=1)
        og[z, y, :, cols] = (grp[z, y, :, 96:97].astype(F32) * scale * value).astype(BF16)
        plan.now += 0.8
        plan.spawn(gather_plane(og, q, 0, grads[q]))

    def to_places(kind):
        swap, due = send(gt.at[kind, :, 1 - c], gt_in.at[kind], sibling, "core")
        yield due
        swap.wait_recv()
        for p in range(nx):
            add_into(gt.at[kind, p, c], gt_in.at[kind, p])
        n = gt.shape[3]
        ends = []
        for h, far in ((0, 1), (1, -1)):
            where = pl.ds(h * (n // 2), n // 2)
            own = lambda p, where=where: gt.at[kind, p, c, where]
            landing = lambda w, where=where: lambda s: gr.at[kind, (1 - w) // 2, s, where]
            ends += both_ways(
                lambda w, end, own=own, landing=landing, far=far: ring_sum(
                    ring_x, w, own, landing(w), end, far, 0.05
                )
            )
        for end in ends:
            yield end
        if kind:
            grad_ref[1] = gt[1, x, c]
        else:
            grad_ref[0] = gt[0, x, c].astype(F32).T.astype(BF16)

    def backward():
        per_part = nx * CORES // n_part
        for q in range(n_part):
            yield grads[q]
            yield Work(1.2)

            @pl.loop(0, per_part)
            def _(k):
                to = q * per_part + k
                cols = pl.ds(pl.multiple_of(to * share, share), share)
                value = dot(hT[...], og[:, :, :, cols].reshape(group, share))
                gt[1, to // CORES, lax.rem(to, CORES)] = value.astype(BF16)

            if q == n_part - 1:
                plan.spawn(to_places(1))
            yield Work(1.2)

            @pl.loop(0, group // step)
            def _(k):
                block = og[pl.ds(k * blocks, blocks), :, :, part_cols(q)].reshape(step, wide)
                place = pl.ds(pl.multiple_of(k * step, step), step)
                value = dot_nt(down[:, part_cols(q)], block)
                if q:
                    value = value + back[:, place]
                if q < n_part - 1:
                    back[:, place] = value
                else:
                    hgT[:, place] = (value * sgT[:, place]).astype(BF16)

        yield Work(2.2)

        @pl.loop(0, nx * CORES)
        def _(k):
            cols = pl.ds(pl.multiple_of(LANES + k * share, LANES), share)
            value = dot(hgT[...], grp[:, :, :, cols].reshape(group, share))
            gt[0, k // CORES, lax.rem(k, CORES)] = value.astype(BF16)

        plan.spawn(to_places(0))

    for q in range(n_part):
        plan.spawn(gather_plane(grp, q, LANES, gathered[q]))
        plan.spawn(take_slots(q))
        plan.spawn(first_product(q))
        plan.spawn(second_product(q))
        plan.spawn(student_output(q))
        plan.spawn(output_grad(q))
    plan.spawn(student_forward())
    plan.spawn(backward())
    plan.run()

    for copy in sent:
        copy.wait_send()


def per_device(nz, ny, nx, tokens, expert_ids, gates, valid, w_in, w_out, up_proj, down_proj):
    tok, width = tokens.shape
    ffw, hidden = w_in.shape[2], up_proj.shape[1]
    group = nz * ny * tok
    slots = nz * ny * CAP
    share = width // (nx * CORES)
    scale = 1.0 / float(group * nx * CORES) ** 0.5
    n_part = 2
    wide = width // n_part
    copies = 384
    vmem = lambda shape, dtype=BF16: pltpu.VMEM(shape, dtype)
    scratch = [
        vmem((width, ffw)), vmem((ffw, width)), vmem((width, hidden)), vmem((hidden, width)),
        vmem((nz, ny, tok, width + LANES)),
        vmem((nx, CORES, slots, width)),
        vmem((nx, CORES, slots, ffw), F32),
        vmem((nx, CORES, slots, ffw)),
        vmem((nx, CORES, slots, width)),
        vmem((nx, slots, width)),
        vmem((n_part, 2, nx // 2, slots, wide)),
        vmem((n_part, nz * ny, CAP * FOLD, wide // FOLD)),
        vmem((n_part, nz * ny, CAP * FOLD, wide // FOLD)),
        vmem((group, hidden)),
        vmem((hidden, group)), vmem((hidden, group), F32), vmem((hidden, group)),
        vmem((hidden, group), F32),
        vmem((nz, ny, tok, width)),
        vmem((ny, 2, nz // 2, tok, wide)),
        vmem((nz, 2, ny // 2, tok, wide)),
        vmem((2, nz // 2, tok, wide)),
        vmem((ny - 1, tok, wide)),
        vmem((nz, ny, tok, width)),
        vmem((2, nx, CORES, hidden, share)),
        vmem((2, nx, hidden, share)),
        vmem((2, 2, nx // 2, hidden, share)),
        pltpu.SemaphoreType.DMA((copies,)),
        pltpu.SemaphoreType.DMA((copies,)),
        pltpu.SemaphoreType.DMA((4,)),
    ]
    in_vmem = pl.BlockSpec(memory_space=pltpu.VMEM)
    anywhere = pl.BlockSpec(memory_space=pl.ANY)
    grads = pl.pallas_call(
        functools.partial(kernel, nz, ny, nx, scale, n_part),
        out_shape=jax.ShapeDtypeStruct((2, share, hidden), BF16),
        in_specs=[in_vmem] * 4 + [anywhere] * 4,
        out_specs=in_vmem,
        scratch_shapes=scratch,
        cost_estimate=pl.CostEstimate(flops=15 * 10**9, bytes_accessed=11 * 10**6, transcendentals=0),
        compiler_params=pltpu.CompilerParams(
            collective_id=0, has_side_effects=True, vmem_limit_bytes=61 * 2**20
        ),
    )(tokens, expert_ids.T, gates.T, valid.reshape(1, tok), w_in, w_out, up_proj, down_proj)
    return grads[0].astype(F32), grads[1].reshape(hidden, share).astype(F32)


def solution(mesh):
    n_expert, n_dp = mesh.shape["expert"], mesh.shape["dp"]
    ny = 4 if n_expert >= 16 else 2
    nz, nx = n_expert // ny, n_dp // CORES
    return jax.shard_map(
        functools.partial(per_device, nz, ny, nx),
        mesh=mesh,
        in_specs=(
            P(("dp", "expert"), None),
            P(("dp", "expert"), None),
            P(("dp", "expert"), None),
            P(("dp", "expert")),
            P("expert", None, "dp"),
            P("expert", "dp", None),
            P(None, "expert"),
            P("expert", None),
        ),
        out_specs=(P("dp", "expert"), P("expert", "dp")),
        check_vma=False,
    )
```

```python
import functools

import jax
import jax.numpy as jnp
from jax import lax
from jax.experimental import pallas as pl
from jax.experimental.pallas import tpu as pltpu
from jax.sharding import PartitionSpec as P

MESH = pl.DeviceIdType.MESH
CORES = 2
SLACK = 3.0
CAP = 4
PLANE_HOPS = (("z1", 1.0), ("z-1", 1.0), ("y1", 0.5), ("y-1", 0.5))
FOLD = 4
LANES = 128
Z_FIRST = 0
F32, BF16 = jnp.float32, jnp.bfloat16


def dot(a, b):
    return jnp.dot(a, b, preferred_element_type=F32)


def dot_nt(a, b):
    return lax.dot_general(a, b, (((1,), (1,)), ((), ())), preferred_element_type=F32)


class Event:
    def __init__(self):
        self.done = False


class Work:
    def __init__(self, us, rank=0):
        self.us, self.rank = us, rank


class Plan:
    RATE, INNER, LATENCY = 100e3, 400e3, 5.0

    def __init__(self):
        self.now, self.busy, self.processes = 0.0, {}, []

    def transfer(self, link, nbytes):
        if link == "plane":
            return max(self.transfer(way, nbytes * hops) for way, hops in PLANE_HOPS) + self.LATENCY
        start = max(self.now, self.busy.get(link, 0.0))
        self.busy[link] = start + nbytes / (self.INNER if link == "core" else self.RATE / CORES)
        return self.busy[link] + self.LATENCY

    def spawn(self, process):
        self.processes.append([process, self.now])

    def run(self):
        while self.processes:
            ready, works, later = [], [], []
            for i, (_, want) in enumerate(self.processes):
                if isinstance(want, Event):
                    if want.done:
                        ready.append((self.now, i))
                elif isinstance(want, Work):
                    works.append((want.rank, i))
                elif want <= self.now:
                    ready.append((want, i))
                else:
                    later.append((want, i))
            if ready:
                i = min(ready)[1]
            elif works:
                i = min(works)[1]
                self.now += self.processes[i][1].us
            else:
                self.now, i = min(later)
            process = self.processes[i]
            try:
                process[1] = next(process[0])
            except StopIteration:
                self.processes.remove(process)


def add_into(a, b):
    a[...] = (a[...].astype(F32) + b[...].astype(F32)).astype(BF16)


def kernel(
    nz, ny, nx, scale, n_part,
    tok_ref, ids_ref, gate_ref, valid_ref, win_hbm, wout_hbm, up_hbm, down_hbm,
    grad_ref,
    win, wout, up, down, grp, rows, acc, hid, part, part_in, xr, ret, got,
    hstu, hT, sgT, hgT, back, mix, zr, yr, zs, ys, og, gt, gt_in, gr,
    send_sem, recv_sem, load_sem,
):
    e, g = lax.axis_index("expert"), lax.axis_index("dp")
    z, y = e // ny, lax.rem(e, ny)
    x, c = g // CORES, lax.rem(g, CORES)
    tok, width = tok_ref.shape
    group = nz * ny * tok
    slots = nz * ny * CAP
    ffw = win.shape[1]
    wide = width // n_part
    share = width // (nx * CORES)

    def at_z(k):
        return (lax.rem(z + k, nz) * ny + y, g)

    def at_y(k):
        return (z * ny + lax.rem(y + k, ny), g)

    def at_x(k):
        return (e, lax.rem(x + k, nx) * CORES + c)

    sibling = (e, x * CORES + 1 - c)
    ring_z, ring_y, ring_x = (nz, z, at_z, "z"), (ny, y, at_y, "y"), (nx, x, at_x, "x")

    loads = [
        pltpu.make_async_copy(win_hbm.at[0], win, load_sem.at[0]),
        pltpu.make_async_copy(up_hbm, up, load_sem.at[1]),
        pltpu.make_async_copy(wout_hbm.at[0], wout, load_sem.at[2]),
        pltpu.make_async_copy(down_hbm, down, load_sem.at[3]),
    ]

    barrier = pltpu.get_barrier_semaphore()
    near = [sibling]
    near += [(lax.rem(e + k, nz * ny), g) for k in range(1, nz * ny)]
    near += [at_x(k) for k in sorted({1, nx - 1})]
    for device in near:
        pl.semaphore_signal(barrier, inc=1, device_id=device, device_id_type=MESH)
    for load in loads:
        load.start()

    row = lax.broadcasted_iota(jnp.int32, (LANES, tok), 0)
    expert, kind = row & 31, row >> 5
    first, second = ids_ref[0:1, :] == expert, ids_ref[1:2, :] == expert
    hot = jnp.where(first | second, 1.0, 0.0)
    before = lax.broadcasted_iota(jnp.int32, (tok, tok), 0) < lax.broadcasted_iota(jnp.int32, (tok, tok), 1)
    rank = dot(hot.astype(BF16), jnp.where(before, 1.0, 0.0).astype(BF16))
    gate = jnp.where(first, gate_ref[0:1, :], 0.0) + jnp.where(second, gate_ref[1:2, :], 0.0)
    high = gate.astype(BF16).astype(F32)
    table = jnp.where(kind == 0, hot * (1.0 + rank), jnp.where(kind == 1, high, gate - high))
    table = jnp.where(kind == 3, valid_ref[...].astype(F32), table)
    grp[z, y, :, 0:LANES] = table.T.astype(BF16)
    grp[z, y, :, LANES : LANES + width] = tok_ref[...]

    pl.semaphore_wait(barrier, len(near))

    plan = Plan()
    sent = []

    def send(src, dst, device, link):
        k = len(sent)
        copy = pltpu.make_async_remote_copy(
            src_ref=src, dst_ref=dst, send_sem=send_sem.at[k], recv_sem=recv_sem.at[k],
            device_id=device, device_id_type=MESH,
        )
        copy.start()
        size = 2
        for n in src.shape:
            size *= n
        sent.append(copy)
        return copy, plan.transfer(link, size)

    def ring_gather(ring, way, region, done, far, arrived=None):
        n, i, at, name = ring
        steps = n // 2 if way == far else n // 2 - 1
        for s in range(1, steps + 1):
            ref = region(lax.rem(i + n - way * (s - 1), n))
            copy, due = send(ref, ref, at(1 if way == 1 else n - 1), name + str(way))
            yield due
            copy.wait_recv()
            if arrived is not None:
                arrived(way * s)
        done.done = True

    def ring_sum(ring, way, own, landing, done, far, us, slack=0.0):
        n, i, at, name = ring
        steps = n // 2 if way == far else n // 2 - 1
        for s in range(1, steps + 1):
            place = lax.rem(i + n + way * (steps - s + 1), n)
            copy, due = send(own(place), landing(s - 1), at(1 if way == 1 else n - 1), name + str(way))
            yield due + slack
            copy.wait_recv()
            add_into(own(lax.rem(i + n + way * (steps - s), n)), landing(s - 1))
            plan.now += us
        done.done = True

    def both_ways(start):
        ends = []
        for way in (1, -1):
            ends.append(Event())
            plan.spawn(start(way, ends[-1]))
        return ends

    def all_of(events, done):
        for event in events:
            yield event
        done.done = True

    def y_then_z(buf, cols, done):
        ends = []

        def along_z(k):
            far = 1 if k in (0, 1) else -1
            region = lambda p: buf.at[p, lax.rem(y + ny - k, ny), :, cols]
            ends.extend(both_ways(lambda w, end: ring_gather(ring_z, w, region, end, far)))

        mine = buf.at[z, y, :, cols]
        hops = sorted(range(1, ny), key=lambda k: min(k, ny - k))
        copies = [(k, *send(mine, mine, at_y(k), "y1" if k <= ny // 2 else "y-1")) for k in hops]
        along_z(0)
        for k, copy, due in copies:
            yield due
            copy.wait_recv()
            along_z(k)
        plan.spawn(all_of(ends, done))

    def z_then_y(buf, cols, done):
        ends = []

        def along_y(k):
            far = 1 if len(ends) % 4 == 0 else -1
            region = lambda p: buf.at[lax.rem(z + nz - k, nz), p, :, cols]
            ends.extend(both_ways(lambda w, end: ring_gather(ring_y, w, region, end, far)))

        region = lambda p: buf.at[p, y, :, cols]
        firsts = both_ways(lambda w, end: ring_gather(ring_z, w, region, end, 1, along_y))
        along_y(0)
        for end in firsts:
            yield end
        plan.spawn(all_of(ends, done))

    def columns(q, shift):
        return pl.ds(q * wide + (shift if q else 0), wide + (0 if q else shift))

    def gather_plane(buf, q, shift, done):
        return (z_then_y if q == Z_FIRST else y_then_z)(buf, columns(q, shift), done)

    def sum_z_then_y(q, cols, done):
        from_y = []

        def along_z(k):
            to = lax.rem(y + k, ny)
            own = lambda p: mix.at[p, to, :, cols]
            landing = lambda w: lambda s: zr.at[k, (1 - w) // 2, s]
            far = 1 if k in (0, 1) else -1
            for end in both_ways(lambda w, end: ring_sum(ring_z, w, own, landing(w), end, far, 0.1, SLACK)):
                yield end
            if k:
                from_y.append(
                    send(mix.at[z, to, :, cols], ys.at[k - 1], at_y(k), "y1" if k <= ny // 2 else "y-1")
                )
            finished[k].done = True

        finished = [Event() for _ in range(ny)]
        for k in sorted(range(ny), key=lambda k: -min(k, ny - k)):
            plan.spawn(along_z(k))
        for event in finished:
            yield event
        for copy, due in from_y:
            yield due
            copy.wait_recv()
        done.done = True

    def sum_y_then_z(q, cols, done):
        finished = [Event() for _ in range(nz)]

        def along_y(k, far):
            to = lax.rem(z + k, nz)
            own = lambda p: mix.at[to, p, :, cols]
            landing = lambda w: lambda s: yr.at[k, (1 - w) // 2, s]
            for end in both_ways(lambda w, end: ring_sum(ring_y, w, own, landing(w), end, far, 0.1, SLACK)):
                yield end
            finished[k].done = True

        def along_z(way, end):
            n, i, at, name = ring_z
            steps = n // 2 if way == 1 else n // 2 - 1
            for s in range(1, steps + 1):
                k = steps - s + 1
                yield finished[(way * k) % n]
                copy, due = send(
                    mix.at[lax.rem(i + n + way * k, n), y, :, cols], zs.at[(1 - way) // 2, s - 1],
                    at(1 if way == 1 else n - 1), name + str(way),
                )
                yield due + SLACK
                copy.wait_recv()
                yield finished[(way * (k - 1)) % n]
                add_into(mix.at[lax.rem(i + n + way * (k - 1), n), y, :, cols], zs.at[(1 - way) // 2, s - 1])
                plan.now += 0.1
            end.done = True

        for at, k in enumerate(sorted(range(nz), key=lambda k: -min(k, nz - k))):
            plan.spawn(along_y(k, 1 if at % 2 == 0 else -1))
        for end in both_ways(along_z):
            yield end
        done.done = True

    each = lambda: [Event() for _ in range(n_part)]
    gathered, selected, hidden, summed, mixed, out, grads = each(), each(), each(), each(), each(), each(), each()
    student = Event()
    part_cols = lambda q: pl.ds(q * wide, wide)
    hops = nx // 2
    order = [nx // 2] + [k for k in range(1, nx) if k != nx // 2] + [0]
    whole = [[Event() for _ in range(nx)] for _ in range(n_part)]
    multiplied = [[Event() for _ in range(nx)] for _ in range(n_part)]

    def take_slots(q):
        if q:
            yield selected[q - 1]
        yield gathered[q]
        pick = jnp.where(lax.broadcasted_iota(jnp.int32, (16, LANES), 1) == e, 1.0, 0.0).astype(BF16)
        ranks_row = dot_nt(pick, grp[:, :, :, 0:LANES].reshape(group, LANES))[0:1, :]
        slot = lax.broadcasted_iota(jnp.int32, (slots, group), 0)
        token = lax.broadcasted_iota(jnp.int32, (slots, group), 1)
        chosen = (slot // CAP == token // tok) & (ranks_row == ((slot & (CAP - 1)) + 1).astype(F32))
        select = jnp.where(chosen, 1.0, 0.0).astype(BF16)
        tile = min(512, wide)
        for j in range(wide // tile):
            at = q * wide + j * tile
            block = grp[:, :, :, LANES + at : LANES + at + tile].reshape(group, tile)
            rows[x, c, :, at : at + tile] = dot(select, block).astype(BF16)
        plan.now += 0.6
        selected[q].done = True
        cols = part_cols(q)
        fromsib = {k: [] for k in range(nx)}
        low, high = pl.ds(0, slots // 2), pl.ds(slots // 2, slots // 2)

        def to_sibling(k, p, where):
            ref = rows.at[p, c, where, cols]
            fromsib[k].append(send(ref, ref, sibling, "core"))
            if len(fromsib[k]) == (2 if k else 1):
                plan.spawn(settle(k))

        def settle(k):
            for copy, due in fromsib[k]:
                yield due
                copy.wait_recv()
            whole[q][k].done = True

        to_sibling(0, x, pl.ds(0, slots))
        for where, far in ((low, 1), (high, -1)):
            region = lambda p, where=where: rows.at[p, c, where, cols]
            both_ways(
                lambda w, end, where=where, region=region, far=far: ring_gather(
                    ring_x, w, region, end, far,
                    lambda d, where=where: to_sibling(d % nx, lax.rem(x + nx - d, nx), where),
                )
            )

    def place_of(k):
        return lax.rem(x + nx - k, nx)

    def first_product(q):
        for k in [0] + [k for k in range(1, nx) if k != hops] + [hops]:
            yield whole[q][k]
            if q:
                yield multiplied[q - 1][k]
            yield Work(1.4)
            if q == 0 and k == 0:
                loads[0].wait()
            p = place_of(k)
            tile = min(256, ffw)

            @pl.loop(0, ffw // tile)
            def _(j):
                cols = pl.ds(pl.multiple_of(j * tile, tile), tile)
                value = dot(
                    rows[p, :, :, part_cols(q)].reshape(CORES * slots, wide), win[part_cols(q), cols]
                ).reshape(CORES, slots, tile)
                if q:
                    value = value + acc[p, :, :, cols]
                if q < n_part - 1:
                    acc[p, :, :, cols] = value
                else:
                    hid[p, :, :, cols] = jnp.maximum(value, 0.0).astype(BF16)

            multiplied[q][k].done = True
        hidden[q].done = True

    def second_product(q):
        yield hidden[n_part - 1]
        if q:
            yield Work(0.0, q)
        if q == 0:
            loads[2].wait()
        tile = min(256, wide)
        for j in range(wide // tile):
            yield Work(1.0, q)
            cols = pl.ds(q * wide + j * tile, tile)
            value = dot(hid[...].reshape(nx * CORES * slots, ffw), wout[:, cols])
            part[:, :, :, cols] = value.astype(BF16).reshape(nx, CORES, slots, tile)
        cols = part_cols(q)
        swaps = []
        for k in order:
            p = lax.rem(x + k, nx)
            swaps.append(send(part.at[p, 1 - c, :, cols], part_in.at[p, :, cols], sibling, "core"))
        for k, (copy, due) in zip(order, swaps):
            p = lax.rem(x + k, nx)
            yield due
            copy.wait_recv()
            add_into(part.at[p, c, :, cols], part_in.at[p, :, cols])
        ends = []
        for h, far in ((0, 1), (1, -1)):
            where = pl.ds(h * (slots // 2), slots // 2)
            own = lambda p, where=where: part.at[p, c, where, cols]
            landing = lambda w, where=where: lambda s: xr.at[q, (1 - w) // 2, s, where]
            ends += both_ways(
                lambda w, end, own=own, landing=landing, far=far: ring_sum(
                    ring_x, w, own, landing(w), end, far, 0.15
                )
            )
        for end in ends:
            yield end
        n_place, fold = nz * ny, wide // FOLD
        i = lax.broadcasted_iota(jnp.int32, (n_place * CAP * FOLD, slots), 0)
        slot = lax.broadcasted_iota(jnp.int32, (n_place * CAP * FOLD, slots), 1)
        at_row = slot == (i >> 4) * CAP + (i & 3)
        folded = jnp.zeros((n_place * CAP * FOLD, fold), F32)
        for f in range(FOLD):
            move = jnp.where(at_row & (((i >> 2) & 3) == f), 1.0, 0.0).astype(BF16)
            folded = folded + dot(move, part[x, c, :, q * wide + f * fold : q * wide + (f + 1) * fold])
        ret[q] = folded.astype(BF16).reshape(n_place, CAP * FOLD, fold)
        got[q, e] = ret[q, e]
        plan.now += 0.8
        backs = []
        for k in range(1, n_place):
            to = lax.rem(e + k, n_place)
            backs.append(send(ret.at[q, to], got.at[q, e], (to, g), "plane"))
        for copy, due in backs:
            yield due
            copy.wait_recv()
        summed[q].done = True

    blocks = 2 if nz % 2 == 0 else 1
    step = blocks * ny * tok

    def student_forward():
        for event in gathered:
            yield event
        loads[1].wait()
        for k in range(group // step):
            yield Work(1.0, 5)
            at = k * step
            block = grp[k * blocks : (k + 1) * blocks, :, :, LANES : LANES + width].reshape(step, width)
            value = dot(block, up[...])
            sig = jax.nn.sigmoid(value)
            act = value * sig
            hstu[at : at + step, :] = act.astype(BF16)
            hT[:, at : at + step] = act.T.astype(BF16)
            sgT[:, at : at + step] = (sig * (1.0 + value * (1.0 - sig))).T
        student.done = True

    def student_output(q):
        yield student
        yield Work(1.2, 6)
        if q == 0:
            loads[3].wait()
        tile = min(512, wide)

        @pl.loop(0, group // step)
        def _(k):
            at = pl.multiple_of(k * step, step)
            for j in range(wide // tile):
                cols = slice(q * wide + j * tile, q * wide + (j + 1) * tile)
                value = dot(hstu[pl.ds(at, step), :], down[:, cols])
                mix[pl.ds(k * blocks, blocks), :, :, cols] = value.astype(BF16).reshape(blocks, ny, tok, tile)

        plan.spawn((sum_y_then_z if q == Z_FIRST else sum_z_then_y)(q, columns(q, 0), mixed[q]))

    def output_grad(q):
        yield mixed[q]
        yield summed[q]
        cols = columns(q, 0)
        value = mix[z, y, :, cols].astype(F32)
        if q != Z_FIRST:
            for k in range(ny - 1):
                value = value + ys[k].astype(F32)
        n_row = nz * ny * CAP * FOLD
        table = grp[z, y, :, 0:LANES]
        line = lax.broadcasted_iota(jnp.int32, (LANES, n_row), 0)
        source = lax.broadcasted_iota(jnp.int32, (LANES, n_row), 1) >> 4
        spread = lambda off: dot(table, jnp.where(line == source + off, 1.0, 0.0).astype(BF16))
        ranks, high, low = spread(0), spread(32), spread(64)
        i = lax.broadcasted_iota(jnp.int32, (tok, n_row), 1)
        named = ranks == ((i & 3) + 1).astype(F32)
        back_rows = got[q].reshape(n_row, wide // FOLD)
        pieces = []
        for f in range(FOLD):
            here = named & (((i >> 2) & 3) == f)
            pieces.append(
                dot(jnp.where(here, high, 0.0).astype(BF16), back_rows)
                + dot(jnp.where(here, low, 0.0).astype(BF16), back_rows)
            )
        value = value - jnp.concatenate(pieces, axis=1)
        og[z, y, :, cols] = (grp[z, y, :, 96:97].astype(F32) * scale * value).astype(BF16)
        plan.now += 0.8
        plan.spawn(gather_plane(og, q, 0, grads[q]))

    def to_places(kind):
        swap, due = send(gt.at[kind, :, 1 - c], gt_in.at[kind], sibling, "core")
        yield due
        swap.wait_recv()
        for p in range(nx):
            add_into(gt.at[kind, p, c], gt_in.at[kind, p])
        n = gt.shape[3]
        ends = []
        for h, far in ((0, 1), (1, -1)):
            where = pl.ds(h * (n // 2), n // 2)
            own = lambda p, where=where: gt.at[kind, p, c, where]
            landing = lambda w, where=where: lambda s: gr.at[kind, (1 - w) // 2, s, where]
            ends += both_ways(
                lambda w, end, own=own, landing=landing, far=far: ring_sum(
                    ring_x, w, own, landing(w), end, far, 0.05
                )
            )
        for end in ends:
            yield end
        if kind:
            grad_ref[1] = gt[1, x, c]
        else:
            grad_ref[0] = gt[0, x, c].astype(F32).T.astype(BF16)

    def backward():
        per_part = nx * CORES // n_part
        for q in range(n_part):
            yield grads[q]
            yield Work(1.2)

            @pl.loop(0, per_part)
            def _(k):
                to = q * per_part + k
                cols = pl.ds(pl.multiple_of(to * share, share), share)
                value = dot(hT[...], og[:, :, :, cols].reshape(group, share))
                gt[1, to // CORES, lax.rem(to, CORES)] = value.astype(BF16)

            if q == n_part - 1:
                plan.spawn(to_places(1))
            yield Work(1.2)

            @pl.loop(0, group // step)
            def _(k):
                block = og[pl.ds(k * blocks, blocks), :, :, part_cols(q)].reshape(step, wide)
                place = pl.ds(pl.multiple_of(k * step, step), step)
                value = dot_nt(down[:, part_cols(q)], block)
                if q:
                    value = value + back[:, place]
                if q < n_part - 1:
                    back[:, place] = value
                else:
                    hgT[:, place] = (value * sgT[:, place]).astype(BF16)

        yield Work(2.2)

        @pl.loop(0, nx * CORES)
        def _(k):
            cols = pl.ds(pl.multiple_of(LANES + k * share, LANES), share)
            value = dot(hgT[...], grp[:, :, :, cols].reshape(group, share))
            gt[0, k // CORES, lax.rem(k, CORES)] = value.astype(BF16)

        plan.spawn(to_places(0))

    for q in range(n_part):
        plan.spawn(gather_plane(grp, q, LANES, gathered[q]))
        plan.spawn(take_slots(q))
        plan.spawn(first_product(q))
        plan.spawn(second_product(q))
        plan.spawn(student_output(q))
        plan.spawn(output_grad(q))
    plan.spawn(student_forward())
    plan.spawn(backward())
    plan.run()

    for copy in sent:
        copy.wait_send()


def per_device(nz, ny, nx, tokens, expert_ids, gates, valid, w_in, w_out, up_proj, down_proj):
    tok, width = tokens.shape
    ffw, hidden = w_in.shape[2], up_proj.shape[1]
    group = nz * ny * tok
    slots = nz * ny * CAP
    share = width // (nx * CORES)
    scale = 1.0 / float(group * nx * CORES) ** 0.5
    n_part = 2
    wide = width // n_part
    copies = 384
    vmem = lambda shape, dtype=BF16: pltpu.VMEM(shape, dtype)
    scratch = [
        vmem((width, ffw)), vmem((ffw, width)), vmem((width, hidden)), vmem((hidden, width)),
        vmem((nz, ny, tok, width + LANES)),
        vmem((nx, CORES, slots, width)),
        vmem((nx, CORES, slots, ffw), F32),
        vmem((nx, CORES, slots, ffw)),
        vmem((nx, CORES, slots, width)),
        vmem((nx, slots, width)),
        vmem((n_part, 2, nx // 2, slots, wide)),
        vmem((n_part, nz * ny, CAP * FOLD, wide // FOLD)),
        vmem((n_part, nz * ny, CAP * FOLD, wide // FOLD)),
        vmem((group, hidden)),
        vmem((hidden, group)), vmem((hidden, group), F32), vmem((hidden, group)),
        vmem((hidden, group), F32),
        vmem((nz, ny, tok, width)),
        vmem((ny, 2, nz // 2, tok, wide)),
        vmem((nz, 2, ny // 2, tok, wide)),
        vmem((2, nz // 2, tok, wide)),
        vmem((ny - 1, tok, wide)),
        vmem((nz, ny, tok, width)),
        vmem((2, nx, CORES, hidden, share)),
        vmem((2, nx, hidden, share)),
        vmem((2, 2, nx // 2, hidden, share)),
        pltpu.SemaphoreType.DMA((copies,)),
        pltpu.SemaphoreType.DMA((copies,)),
        pltpu.SemaphoreType.DMA((4,)),
    ]
    in_vmem = pl.BlockSpec(memory_space=pltpu.VMEM)
    anywhere = pl.BlockSpec(memory_space=pl.ANY)
    grads = pl.pallas_call(
        functools.partial(kernel, nz, ny, nx, scale, n_part),
        out_shape=jax.ShapeDtypeStruct((2, share, hidden), BF16),
        in_specs=[in_vmem] * 4 + [anywhere] * 4,
        out_specs=in_vmem,
        scratch_shapes=scratch,
        cost_estimate=pl.CostEstimate(flops=15 * 10**9, bytes_accessed=11 * 10**6, transcendentals=0),
        compiler_params=pltpu.CompilerParams(
            collective_id=0, has_side_effects=True, vmem_limit_bytes=61 * 2**20
        ),
    )(tokens, expert_ids.T, gates.T, valid.reshape(1, tok), w_in, w_out, up_proj, down_proj)
    return grads[0].astype(F32), grads[1].reshape(hidden, share).astype(F32)


def solution(mesh):
    n_expert, n_dp = mesh.shape["expert"], mesh.shape["dp"]
    ny = 4 if n_expert >= 16 else 2
    nz, nx = n_expert // ny, n_dp // CORES
    return jax.shard_map(
        functools.partial(per_device, nz, ny, nx),
        mesh=mesh,
        in_specs=(
            P(("dp", "expert"), None),
            P(("dp", "expert"), None),
            P(("dp", "expert"), None),
            P(("dp", "expert")),
            P("expert", None, "dp"),
            P("expert", "dp", None),
            P(None, "expert"),
            P("expert", None),
        ),
        out_specs=(P("dp", "expert"), P("expert", "dp")),
        check_vma=False,
    )
```
